512 devices in a mesh: band: 128 (over y, z, core), chan: 4 (over x).
Axes of the slice: x: 4, y: 8, z: 8, core: 2. Of those that a mesh axis runs over, the one named last changes fastest.
Arguments:
- atmos: bfloat16 [12, 512, 1440], P('chan', 'band'), may hold values from -6 to 6
- remap_lat: bfloat16 [32768, 64, 4], P('band'), may hold values from -3 to 3
- remap_lon: bfloat16 [32768, 32, 64], P('band'), may hold values from -0.09375 to 0.09375
- pair_tile: int32 [32768, 1], P('band'), may hold values from 0 to 255; in each aligned block of 256 rows (0 to 255, 256 to 511, ...) at most 2 rows name the same one
- pair_col: int32 [32768], P('band'), may hold values from 0 to 1408
- tile_owner: int32 [256], replicated, may hold values from 0 to 255, each once
- neighbours: int32 [256, 4], replicated, may hold values from -1 to 255, as said below
- land_mask: int32 [256, 4096], P('band'), may hold values 0 or 1
- stem_w: bfloat16 [12, 192], P(None, 'chan'), may hold values from -1.75 to 1.75
- dw_w: bfloat16 [192, 49], P('chan'), may hold values from -0.875 to 0.875
- ln_gain: bfloat16 [192], P('chan'), may hold values from 0.099609375 to 1.8984375
- w_in: bfloat16 [768, 192], P('chan'), may hold values from -0.4375 to 0.4375
- b_in: bfloat16 [768], P('chan'), may hold values from -3 to 3
- w_out: bfloat16 [768, 192], P('chan'), may hold values from -0.21875 to 0.21875
- head_w: bfloat16 [192], P('chan'), may hold values from -0.4375 to 0.4375
Outputs:
- sst: float32 [256, 4096], P('band')
The draws below stay inside these ranges and needn't reach their ends.
Inputs may be any that keep to these rules, and one draw needn't show every extreme that they name: `pair_tile`: the pairs of one band device (aligned blocks of 256 rows) name any one tile at most 2 times; every tile is named by some pair. `tile_owner`: each place once. `neighbours`: tiles form a grid of 4 rows of 64 tiles that closes west to east; -1 only north of the first row and south of the last; if u is the north neighbour of t then t is the south neighbour of u, and likewise west and east.
All inputs are finite; a program needn't handle non-finite values. No bound on the sum of `land_mask` on one device may be relied on, other than what follows from the above.
Results may differ from the reference program's by a relative error of at most 0.023.
Values may be sent and summed in bfloat16 or wider, within the bound.
A program may use at most 64 MiB of HBM per device.

```python
import math
import jax
import jax.numpy as jnp
import numpy as np
from jax import lax

FIELDS = 12
ATM_LON = 1440
ROWS_DEV = 4
AC = 32
TS = 64
TILES_DEV = 2
PAIRS_DEV = 256
WIDTH = 192
FFN = 768
CAP = 2
TILES = 256
ATM_ROWS = 512
N_BAND = 128
N_CHAN = 4


def draw_neighbours(key, part):
    key = jax.random.fold_in(key, 7)
    ordering = jax.random.permutation(key, TILES).astype(jnp.int32)
    across = TILES // 4
    positions = jnp.arange(TILES, dtype=jnp.int32)
    grid_row = positions // across
    grid_col = positions % across
    northward = jnp.where(grid_row > 0, ordering[jnp.maximum(positions - across, 0)], -1)
    southward = jnp.where(grid_row < 3, ordering[jnp.minimum(positions + across, TILES - 1)], -1)
    westward = ordering[grid_row * across + (grid_col + across - 1) % across]
    eastward = ordering[grid_row * across + (grid_col + 1) % across]
    lookup_table = jnp.stack([northward, southward, westward, eastward], axis=1).astype(jnp.int32)
    return jnp.zeros((TILES, 4), jnp.int32).at[ordering].set(lookup_table)


def with_ends(drawn, key, low, largest):
    shape = drawn.shape
    index_at = [jax.random.randint(jax.random.fold_in(key, axis), (), 0, shape[axis]) for axis in range(len(shape))]
    drawn = drawn.at[tuple(index_at)].set(low)
    longest = shape.index(max(shape))
    index_at[longest] = (index_at[longest] + 1) % shape[longest]
    return drawn.at[tuple(index_at)].set(largest)


def levels(key, dims, cuts, smallest, high):
    level = 1.0
    for axis_at, blocks in cuts:
        draws = jax.random.uniform(jax.random.fold_in(jax.random.fold_in(key, 6), axis_at), (blocks,), jnp.float32, smallest / len(cuts), high / len(cuts))
        level = level * jnp.repeat(jnp.exp(draws), dims[axis_at] // blocks).reshape((-1,) + (1,) * (len(dims) - 1 - axis_at))
    return level


def deal_out(rng, own, number, rows, count, top, bound, lean):
    ranking = jax.random.permutation(rng, count)
    packed, common = portions_of(count, rows * top, bound, lean, True), portions_of(count, rows * top, bound, lean, False)
    places = jnp.arange(count)

    def named(tallies, rotation):
        used = int((tallies > 0).sum())
        fixed = max(1, used // 4)
        shifted = fixed + (places - fixed + rotation * (used - fixed)) % max(1, count - fixed)
        return jnp.zeros((count,), jnp.int32).at[ranking[jnp.where(places < fixed, places, shifted)]].set(jnp.asarray(tallies, jnp.int32))

    tallies = jnp.where(number % 4 == 0, named(packed, number // 4), named(common, number - number // 4 - 1))
    mixed = jax.random.permutation(jax.random.fold_in(own, 3), count)
    giver, sink = mixed[0:count // 2 * 2:2], mixed[1:count // 2 * 2:2]
    margin = jnp.minimum(tallies[giver] - 1, bound - tallies[sink]) // 2
    margin = jnp.where((giver == ranking[0]) | (sink == ranking[0]) | (tallies[sink] == 0), 0, jnp.maximum(margin, 0))
    shifted = jax.random.randint(jax.random.fold_in(own, 4), (count // 2,), 0, 1 << 20) % (margin + 1)
    tallies = tallies.at[giver].add(-shifted).at[sink].add(shifted)
    members = jnp.searchsorted(jnp.cumsum(tallies), jnp.arange(rows * top), side="right").astype(jnp.int32)
    table = members.reshape(top, rows).T
    table = table[jax.random.permutation(jax.random.fold_in(own, 1), rows)]
    rotation = jax.random.randint(jax.random.fold_in(own, 2), (rows, 1), 0, top)
    return jnp.take_along_axis(table, (jnp.arange(top)[None, :] + rotation) % top, axis=1)


def portions_of(amount, total, limit, skew, full):
    portions = [(1 << 20) // math.isqrt(rank ** skew) + 1 for rank in range(1, amount + 1)]
    largest = limit if full else min(limit, max(-(-total // amount), total * portions[0] // sum(portions)))
    least = 1 if total - largest >= amount - 1 else 0
    holding, spare = [largest] + [least] * (amount - 1), total - largest - least * (amount - 1)
    while spare > 0:
        movable = [i for i in range(1, amount) if holding[i] < largest] or [i for i in range(1, amount) if holding[i] < limit]
        mass, left = sum([portions[i] for i in movable]), spare
        for i in movable:
            extra = min(limit - holding[i], max(1, left * portions[i] // mass), spare)
            holding[i] = holding[i] + extra
            spare = spare - extra
    return np.array(holding)


def noise(own_key, dims, scale, bound, shards=(), kind=jnp.bfloat16):
    values = jax.random.normal(own_key, dims, jnp.float32) * scale
    if len(shards) > 0:
        values = levels(own_key, dims, shards, -0.22, 0.18) * values
    return jnp.clip(values, min=-bound, max=bound).astype(kind)


def setup_inputs(seed: int = 0) -> dict:
    keys = jax.random.split(jax.random.key(seed), 16)
    atmos = noise(keys[0], (FIELDS, ATM_ROWS, ATM_LON), 1.0, 6.0, ((0, 4), (1, 128)))
    remap_lat = noise(keys[1], (N_BAND * PAIRS_DEV, TS, ROWS_DEV), ROWS_DEV ** -0.5, 3.0, ((0, 128),))
    remap_lon = noise(keys[2], (N_BAND * PAIRS_DEV, AC, TS), (AC * PAIRS_DEV // TILES_DEV) ** -0.5, 0.09375, ((0, 128),))
    pair_tile_keys = jax.random.split(jax.random.fold_in(keys[3], 1), (N_BAND * PAIRS_DEV) // PAIRS_DEV)
    pair_tile_turns = jax.random.permutation(jax.random.fold_in(keys[3], 3), (N_BAND * PAIRS_DEV) // PAIRS_DEV)
    pair_tile = jax.vmap(lambda own, number: deal_out(jax.random.fold_in(keys[3], 2), own, number, PAIRS_DEV, TILES, 1, CAP, 2))(pair_tile_keys, pair_tile_turns).reshape((N_BAND * PAIRS_DEV, 1))
    pair_col = with_ends(jax.random.randint(keys[4], (N_BAND * PAIRS_DEV,), 0, ATM_LON - AC + 1), jax.random.fold_in(keys[4], 1), 0, ATM_LON - AC).astype(jnp.int32)
    tile_owner = jax.random.permutation(keys[5], TILES).astype(jnp.int32)
    neighbours = draw_neighbours(jax.random.fold_in(keys[15], 71), 0)
    land_mask = with_ends((jax.random.randint(keys[7], (TILES, TS * TS), 0, 4) < 3).astype(jnp.int32), jax.random.fold_in(keys[7], 1), 0, 1)
    stem_w = noise(keys[8], (FIELDS, WIDTH), FIELDS ** -0.5, 1.75, ((1, 4),))
    dw_w = noise(keys[9], (WIDTH, 49), 49 ** -0.5, 0.875, ((0, 4),))
    ln_gain = jnp.clip(1.0 + 0.18 * jax.random.normal(keys[10], (WIDTH,), jnp.float32), 0.099609375, 1.8984375).astype(jnp.bfloat16)
    w_in = noise(keys[11], (FFN, WIDTH), WIDTH ** -0.5, 0.4375, ((0, 4),))
    b_in = noise(keys[12], (FFN,), 0.5, 3.0, ((0, 4),))
    w_out = noise(keys[13], (FFN, WIDTH), FFN ** -0.5, 0.21875, ((0, 4),))
    head_w = noise(keys[14], (WIDTH,), WIDTH ** -0.5, 0.4375, ((0, 4),))
    return dict(atmos=atmos, remap_lat=remap_lat, remap_lon=remap_lon, pair_tile=pair_tile, pair_col=pair_col, tile_owner=tile_owner, neighbours=neighbours, land_mask=land_mask, stem_w=stem_w, dw_w=dw_w, ln_gain=ln_gain, w_in=w_in, b_in=b_in, w_out=w_out, head_w=head_w)


def depthwise(features, kernel, side):
    wide = side + 6
    flat_rows = jnp.pad(features.astype(jnp.float32), ((0, 0), (0, 0), (0, 8)))
    total = jnp.zeros((features.shape[0], features.shape[1], side * wide), jnp.float32)
    for row_shift in range(7):
        for col_shift in range(7):
            offset = row_shift * wide + col_shift
            weight_col = kernel[:, row_shift * 7 + col_shift].astype(jnp.float32)
            total = total + weight_col[:, None, None] * flat_rows[:, :, offset:offset + side * wide]
    total = total.reshape(features.shape[0], features.shape[1], side, wide)[..., :side]
    return total.reshape(features.shape[0], features.shape[1], side * side)

def assemble(fluxes, above, below, lefts, rights):
    middle = jnp.concatenate([lefts, fluxes, rights], axis=-1)
    top_rows = jnp.pad(above, ((0, 0), (0, 0), (0, 0), (3, 3)))
    bottom_rows = jnp.pad(below, ((0, 0), (0, 0), (0, 0), (3, 3)))
    return jnp.concatenate([top_rows, middle, bottom_rows], axis=2)

def layer_norm(mixed, gain):
    values = mixed.astype(jnp.float32)
    mean_val = lax.optimization_barrier(jnp.sum(values, axis=0)) / WIDTH
    mean_sq = lax.optimization_barrier(jnp.sum(values * values, axis=0)) / WIDTH
    variance = mean_sq - mean_val * mean_val
    scaled = (values - mean_val[None, :]) * lax.rsqrt(variance + 1e-06)[None, :]
    return (scaled * gain.astype(jnp.float32)[:, None]).astype(jnp.bfloat16)

def remap_all(atmos, remap_lat, remap_lon, pair_tile, pair_col, tile_owner):
    places = tile_owner[pair_tile[:, 0]]
    zero_index = jnp.int32(0)

    def one_band(accum, band_id):
        band_rows = lax.dynamic_slice_in_dim(atmos, band_id * ROWS_DEV, ROWS_DEV, 1)
        columns = lax.dynamic_slice_in_dim(pair_col, band_id * PAIRS_DEV, PAIRS_DEV, 0)
        lat_blocks = lax.dynamic_slice_in_dim(remap_lat, band_id * PAIRS_DEV, PAIRS_DEV, 0)
        lon_blocks = lax.dynamic_slice_in_dim(remap_lon, band_id * PAIRS_DEV, PAIRS_DEV, 0)
        targets = lax.dynamic_slice_in_dim(places, band_id * PAIRS_DEV, PAIRS_DEV, 0)
        windows = jax.vmap(lambda start_col: lax.dynamic_slice(band_rows, (zero_index, zero_index, start_col), (FIELDS, ROWS_DEV, AC)))(columns)
        partial_rows = jnp.einsum('pfrc,pcj->pfrj', windows.astype(jnp.float32), lon_blocks.astype(jnp.float32), precision=lax.Precision.HIGHEST)
        blocks = jnp.einsum('pir,pfrj->pfij', lat_blocks.astype(jnp.float32), partial_rows, precision=lax.Precision.HIGHEST)
        return (accum.at[targets].add(blocks), None)
    start = jnp.zeros((TILES, FIELDS, TS, TS), jnp.float32)
    remapped, unused = lax.scan(one_band, start, jnp.arange(N_BAND, dtype=jnp.int32))
    return remapped

def one_tile(framed, mask_row, stem_w, dw_w, ln_gain, w_in, b_in, w_out, head_w):
    wide = TS + 6
    fields = framed.reshape(FIELDS, wide * wide).astype(jnp.float32)
    features = jnp.einsum('fp,fc->cp', fields, stem_w.astype(jnp.float32), precision=lax.Precision.HIGHEST).astype(jnp.bfloat16)
    mixed = depthwise(features[:, None, :], dw_w, TS)[:, 0, :].astype(jnp.bfloat16)
    inner = features.reshape(WIDTH, wide, wide)[:, 3:3 + TS, 3:3 + TS].reshape(WIDTH, TS * TS)
    normed = layer_norm(mixed, ln_gain)
    before = jnp.dot(w_in, normed, preferred_element_type=jnp.float32) + b_in.astype(jnp.float32)[:, None]
    activated = jax.nn.gelu(before).astype(jnp.bfloat16)
    group = FFN // N_CHAN
    terms = jnp.einsum('khc,khp->kcp', w_out.reshape(N_CHAN, group, WIDTH).astype(jnp.float32), activated.reshape(N_CHAN, group, TS * TS).astype(jnp.float32), precision=lax.Precision.HIGHEST).astype(jnp.bfloat16)
    down = lax.optimization_barrier(jnp.sum(terms.astype(jnp.float32), axis=0))
    state = inner.astype(jnp.float32) + down
    return lax.optimization_barrier(jnp.sum(head_w.astype(jnp.float32)[:, None] * state, axis=0)) * mask_row

def reference(atmos, remap_lat, remap_lon, pair_tile, pair_col, tile_owner, neighbours, land_mask, stem_w, dw_w, ln_gain, w_in, b_in, w_out, head_w):
    remapped = remap_all(atmos, remap_lat, remap_lon, pair_tile, pair_col, tile_owner)
    mask_all = land_mask.astype(jnp.float32)
    fluxes = (remapped * mask_all.reshape(TILES, 1, TS, TS)).astype(jnp.bfloat16)
    tile_at = jnp.zeros((TILES,), jnp.int32).at[tile_owner].set(jnp.arange(TILES, dtype=jnp.int32))
    near_ids = neighbours[tile_at]
    valid = near_ids >= 0
    near_places = tile_owner[jnp.maximum(near_ids, 0)]

    def pick(side_id, strip):
        keep = valid[:, side_id][:, None, None, None]
        return jnp.where(keep, strip[near_places[:, side_id]], jnp.zeros_like(strip))
    above = pick(0, fluxes[:, :, TS - 3:, :])
    below = pick(1, fluxes[:, :, :3, :])
    lefts = pick(2, fluxes[:, :, :, TS - 3:])
    rights = pick(3, fluxes[:, :, :, :3])
    framed = assemble(fluxes, above, below, lefts, rights)

    def per_tile(items):
        return one_tile(items[0], items[1], stem_w, dw_w, ln_gain, w_in, b_in, w_out, head_w)
    return lax.map(per_tile, (framed, mask_all))
```

```python
import functools

import jax
import jax.numpy as jnp
from jax import lax
from jax.experimental import pallas as pl
from jax.experimental.pallas import tpu as pltpu
from jax.sharding import PartitionSpec as P

MESH = pl.DeviceIdType.MESH
F32 = jnp.float32
BF16 = jnp.bfloat16
NX = 4
CORES = 2


def iota(shape, axis):
    return lax.broadcasted_iota(jnp.int32, shape, axis)


def onehot(mask):
    return jnp.where(mask, 1.0, 0.0).astype(BF16)


def mm(a, b):
    return lax.dot_general(a, b, (((1,), (0,)), ((), ())), preferred_element_type=F32)


def mm_nt(a, b):
    return lax.dot_general(a, b, (((1,), (1,)), ((), ())), preferred_element_type=F32)


def mm_tn(a, b):
    return lax.dot_general(a, b, (((0,), (0,)), ((), ())), preferred_element_type=F32)


def third(v):
    return jnp.where(v >= 6, 2, jnp.where(v >= 3, 1, 0))


def kernel(
    side,
    ints,
    atm,
    lat,
    lon,
    mask,
    stem_w,
    dw_w,
    small,
    w_in,
    w_out,
    out,
    xw,
    pls,
    send,
    recv,
    agg,
    part,
    flux,
    stacked,
    strips,
    gath,
    kmats,
    msgs,
    rb,
    fx,
    dmat,
    smat,
    rowsel,
    yx,
    zbuf,
    shift_all,
    w_all,
    o_all,
    c_loc,
    c_all,
    s_loc,
    s_all,
    sm_all,
    winp,
    bcol,
    vcol,
    hcol,
    res,
    p1_send,
    p1_recv,
    p2_send,
    p2_recv,
    a_send,
    a_recv,
    x_send,
    x_recv,
    b_send,
    b_recv,
    w_send,
    w_recv,
    f_send,
    f_recv,
    loc_sem,
):
    n = side
    group = n * CORES
    band = lax.axis_index("band")
    x = lax.axis_index("chan")
    y = band // group
    zc = lax.rem(band, group)
    z = zc // CORES
    c = lax.rem(zc, CORES)
    mine = (zc, y * CORES + c)
    ring = (y, z)

    def band_at(yy, zz, cc):
        return (yy * n + zz) * CORES + cc

    def group_band(k, idx):
        if k == 0:
            return y * group + idx
        return band_at(idx // CORES, z, lax.rem(idx, CORES))

    def ring_band(k, t):
        return band_at(t, z, c) if k == 0 else band_at(y, t, c)

    def remote(src, dst, ssem, rsem, tb, tx):
        return pltpu.make_async_remote_copy(
            src_ref=src,
            dst_ref=dst,
            send_sem=ssem,
            recv_sem=rsem,
            device_id={"band": tb, "chan": tx},
            device_id_type=MESH,
        )

    barrier = pltpu.get_barrier_semaphore()

    def greet(tb, tx):
        pl.semaphore_signal(
            barrier, inc=1, device_id={"band": tb, "chan": tx}, device_id_type=MESH
        )

    @pl.loop(1, group)
    def _(d):
        greet(y * group + lax.rem(zc + d, group), x)

    @pl.loop(1, n)
    def _(d):
        yy = lax.rem(y + d, n)
        greet(band_at(yy, z, 0), x)
        greet(band_at(yy, z, 1), x)

    @pl.loop(1, NX)
    def _(dx):
        xx = lax.rem(x + dx, NX)
        greet(band, xx)

        @pl.loop(1, n)
        def _(d):
            greet(band_at(lax.rem(y + d, n), z, c), xx)
            greet(band_at(y, lax.rem(z + d, n), c), xx)

    pairs = lon.shape[2]
    tiles = pairs
    owner = ints[0:1, :]
    tile = ints[1:2, :]
    col = ints[2:3, :]
    nq = atm.shape[1]
    quot = col // 32
    shift = lax.rem(col, 32)
    qi = iota((nq, pairs), 0)
    blocks0 = mm(atm[...], onehot(qi == quot)).reshape(32, 16, pairs)
    blocks1 = mm(atm[...], onehot(qi == quot + 1)).reshape(32, 16, pairs)
    rows = [blocks0[i] for i in range(32)] + [blocks1[i] for i in range(32)]
    for bit in (16, 8, 4, 2, 1):
        on = jnp.broadcast_to(lax.rem(shift // bit, 2) == 1, (16, pairs))
        count = len(rows) - bit
        rows = [jnp.where(on, rows[i + bit], rows[i]) for i in range(count)]
    for i in range(32):
        xw[i] = rows[i]

    half = min(128, pairs)
    for ph in range(pairs // half):
        for jb in range(2):

            def step(ci, accs):
                block = lon[ci, jb * 32 : jb * 32 + 32, ph * half : (ph + 1) * half].astype(F32)
                return tuple(
                    accs[fr] + xw[ci, fr : fr + 1, ph * half : (ph + 1) * half] * block
                    for fr in range(12)
                )

            accs = lax.fori_loop(
                0, 32, step, tuple(jnp.zeros((32, half), F32) for _ in range(12)), unroll=4
            )
            for f in range(3):
                for r in range(4):
                    pls[r, f * 64 + jb * 32 : f * 64 + jb * 32 + 32, ph * half : (ph + 1) * half] = (
                        accs[f * 4 + r].astype(BF16)
                    )
    for r in range(4):
        pls[r, 192:256, :] = lat[r]

    ti = iota((tiles, pairs), 0)
    named = onehot(ti == tile)
    owner16 = jnp.broadcast_to(owner, (16, tiles)).astype(F32).astype(BF16)
    place = mm(owner16, named)[0:1, :].astype(jnp.int32)
    same = mm_tn(named, named)
    earlier = iota((pairs, pairs), 0) < iota((pairs, pairs), 1)
    rank = jnp.sum(jnp.where(earlier, same, 0.0), axis=0, keepdims=True).astype(jnp.int32)
    kk = lax.rem(place, 2)
    to_band = place // 2
    to_y = to_band // group
    to_zc = lax.rem(to_band, group)
    to_z = to_zc // CORES
    to_c = lax.rem(to_zc, CORES)
    slot = jnp.where(
        kk == 0,
        (to_zc * n + to_y) * 2 + rank,
        ((group + to_y * CORES + to_c) * n + to_z) * 2 + rank,
    )
    slots = 2 * group * n * 2
    perm = onehot(iota((slots, pairs), 0) == slot)
    for r in range(4):
        send[:, r] = mm_nt(perm, pls[r]).astype(BF16).reshape(2 * group, 2 * n, 256)

    greetings = (group - 1) + 2 * (n - 1) + 3 * (2 * n - 1)
    pl.semaphore_wait(barrier, greetings)

    def p1(k, d):
        idx = lax.rem(mine[k] + d, group)
        return remote(
            send.at[k * group + idx],
            recv.at[k, mine[k]],
            p1_send.at[k, idx],
            p1_recv.at[k, mine[k]],
            group_band(k, idx),
            x,
        )

    def p1_in(k, d):
        idx = lax.rem(mine[k] + d, group)
        return remote(
            send.at[k * group + idx],
            recv.at[k, idx],
            p1_send.at[k, idx],
            p1_recv.at[k, idx],
            group_band(k, idx),
            x,
        )

    @pl.loop(1, group)
    def _(d):
        p1(0, d).start()
        p1(1, d).start()

    for k in range(2):
        recv[k, mine[k]] = send[k * group + mine[k]]

    wide = 49 * 16
    lane = iota((49, wide), 1)
    spread = onehot(iota((49, wide), 0) == lane // 16)
    fields = onehot(iota((12, wide), 0) == lax.rem(iota((12, wide), 1), 16))
    combined = mm(dw_w[...], spread) * mm_tn(stem_w[...], fields)
    c_loc[...] = combined.astype(BF16)
    s_loc[...] = mm_tn(stem_w[...], onehot(iota((12, 16), 0) == iota((12, 16), 1))).astype(BF16)
    shares = ((w_in, w_all), (w_out, o_all), (c_loc, c_all), (s_loc, s_all), (small, sm_all))

    def share(i, dx):
        src, dst = shares[i]
        xx = lax.rem(x + dx, NX)
        return remote(src, dst.at[x], w_send.at[i, dx], w_recv.at[i, x], band, xx)

    def share_in(i, dx):
        src, dst = shares[i]
        xx = lax.rem(x + dx, NX)
        return remote(src, dst.at[xx], w_send.at[i, dx], w_recv.at[i, xx], band, xx)

    for dx in range(1, NX):
        for i in (4, 2, 3, 1, 0):
            share(i, dx).start()
    for src, dst in shares:
        dst[x] = src[...]

    ui = iota((tiles, tiles), 0)
    owner1 = jnp.broadcast_to(owner + 1, (16, tiles)).astype(F32).astype(BF16)
    near_rows = [mm(owner1, onehot(ui == ints[3 + s : 4 + s, :]))[0:1, :] for s in range(4)]
    near = jnp.concatenate(near_rows + [jnp.zeros((12, tiles), F32)], axis=0).astype(BF16)
    near_at = mm_nt(near, onehot(ui == owner)).astype(BF16)
    mrows = n * NX * 16
    mcols = group * 32
    mr = iota((mrows, tiles), 0)
    mt, mx, mrho = mr // 64, lax.rem(mr // 16, NX), lax.rem(mr, 16)
    ci = iota((mrows, mcols), 1)
    rho = lax.rem(iota((mrows, mcols), 0), 16)
    to_h = lax.rem(iota((mrows, mcols), 0) // 16, 2)
    src, src_half, src_rho = ci // 32, lax.rem(ci // 16, 2), lax.rem(ci, 16)
    for k in range(2):
        to_place = 2 * (ring_band(k, mt)) + mx // 2
        cols = mm_nt(onehot(iota((mrows, tiles), 1) == to_place), near_at).astype(jnp.int32)
        if k == 0:
            src_place = 2 * (y * group + src)
        else:
            src_place = 2 * band_at(src // CORES, z, lax.rem(src, CORES)) + 1
        src_tag = jnp.where(src_rho == rho, src_place + 1, -1)
        col_ns = jnp.where(to_h == 0, cols[:, 0:1], cols[:, 1:2])
        col_we = jnp.where(rho < 9, cols[:, 2:3], cols[:, 3:4])
        half_we = jnp.where(rho < 9, 0, 1)
        kmats[k, 0] = onehot((col_ns == src_tag) & (src_half == to_h))
        kmats[k, 1] = onehot((col_we == src_tag) & (src_half == half_we))

    h = lax.rem(x, 2)
    frows = 38 * 16
    fr_row = iota((frows, 640), 0)
    r_row, f_row = fr_row // 16, lax.rem(fr_row, 16)
    fx_row = f_row // 3
    fl_row = f_row - 3 * fx_row
    strip_a = jnp.where(h == 0, r_row, r_row - 35)
    in_strip = (strip_a >= 0) & (strip_a <= 2)
    want = jnp.where(
        in_strip,
        576 + fx_row * 16 + fl_row * 3 + strip_a,
        f_row * 48 + jnp.where(h == 0, r_row - 3, r_row + 13),
    )
    smat[...] = onehot((want == iota((frows, 640), 1)) & (f_row < 12))
    rr = iota((frows, 128), 0) // 16
    ff = lax.rem(iota((frows, 128), 0), 16)
    ll = iota((frows, 128), 1)
    cell = rr - 3 + 32 * h
    rowsel[0] = onehot((cell == lax.rem(ll, 64)) & (cell >= 0) & (cell < 64))
    lo = ll < 64
    lx, lrho = lax.rem(ll, 64) // 16, lax.rem(ll, 16)
    fa = jnp.where(lo, lrho - 9, jnp.where(lrho < 9, lrho, lrho - 2))
    ok = (lo & (lrho >= 9)) | (jnp.logical_not(lo) & (lrho < 11))
    rowsel[1] = onehot(ok & (3 * lx + third(fa) == ff))
    kr = iota((128, 128), 0)
    klo = kr < 64
    krho = lax.rem(kr, 16)
    kfa = jnp.where(klo, krho - 9, jnp.where(krho < 9, krho, krho - 2))
    kwest = jnp.logical_not(klo) & (krho < 9)
    lane_to = jnp.where(kwest, 64, 67) + kfa - 3 * third(kfa)
    collapse = onehot(lane_to == iota((128, 128), 1))
    ar = iota((256, 896), 0)
    al = lax.rem(ar, 128)
    ncol = jnp.where(al < 64, al + 3, jnp.where(al < 67, al - 64, jnp.where(al < 70, al, -999)))
    bc = iota((256, 896), 1)
    shift_all[...] = onehot(
        (ar // 128 == lax.rem(bc, 128) // 64) & (ncol == lax.rem(bc, 64) + bc // 128)
    )
    dmat[...] = jnp.zeros(dmat.shape, BF16)
    sr = iota((32, 192), 0)
    sl = iota((32, 192), 1)
    srho = lax.rem(sr, 16)
    sfl = third(srho)
    sa = srho - 3 * sfl
    pick_rows = onehot(
        (srho < 9) & (sl // 64 == sfl) & (lax.rem(sl, 64) == sa + jnp.where(sr < 16, 61, 0))
    )
    er = iota((48, 192), 0)
    el = iota((48, 192), 1)
    erho = lax.rem(er, 16)
    efa = jnp.where(er < 16, erho, jnp.where(er < 32, erho - 9, erho - 2))
    eok = (
        ((er < 16) & (erho < 9))
        | ((er >= 16) & (er < 32) & (erho >= 9))
        | ((er >= 32) & (erho >= 9) & (erho < 11))
    )
    efl = third(efa)
    ea = efa - 3 * efl + jnp.where(er < 16, 61, 0)
    pick_cols = onehot(eok & (el // 64 == efl) & (lax.rem(el, 64) == ea))

    def p2(k, d):
        t = lax.rem(ring[k] + d, n)
        return remote(
            agg.at[k, t],
            part.at[k, ring[k]],
            p2_send.at[k, t],
            p2_recv.at[k, ring[k]],
            ring_band(k, t),
            x,
        )

    def p2_in(k, d):
        t = lax.rem(ring[k] + d, n)
        return remote(
            agg.at[k, t],
            part.at[k, t],
            p2_send.at[k, t],
            p2_recv.at[k, t],
            ring_band(k, t),
            x,
        )

    krows = group * 8 * n
    k_tile = lax.rem(iota((64, krows), 1) // 2, n)
    for k in range(2):

        @pl.loop(1, group)
        def _(d):
            p1_in(k, d).wait_recv()

        got = recv[k].reshape(krows, 256)
        lat_t = got[:, 128:256].astype(F32).T[64:128, :]
        lhs = jnp.concatenate(
            [jnp.where(k_tile == t, lat_t, 0.0).astype(BF16) for t in range(n)], axis=0
        )
        agg[k] = mm(lhs, got[:, 0:192]).astype(BF16).reshape(n, 64, 192)

        @pl.loop(1, n)
        def _(d):
            p2(k, d).start()

        part[k, ring[k]] = agg[k, ring[k]]

    for dx in range(1, NX):
        for i in range(5):
            share_in(i, dx).wait_recv()
    gains = jnp.zeros((16, 192), F32)
    for i in range(NX):
        put = onehot(iota((256, 192), 1) == jnp.where(iota((256, 192), 0) < 48, iota((256, 192), 0) + 48 * i, -1))
        gains = gains + mm(sm_all[i], put)
    row2 = onehot(iota((16, 128), 0) == 2)
    row0 = onehot(iota((16, 128), 0) == 0)
    head = mm_tn(gains.astype(BF16), row2)
    hcol[...] = head
    for i in range(NX):
        blk = pl.ds(i * 192, 192)
        winp[blk, :] = (w_all[i].astype(F32) * gains[1:2, :]).astype(BF16)
        bcol[blk, :] = mm_tn(sm_all[i, :, 0:192], row0)
        vcol[blk, :] = 0.5 * mm(o_all[i], head.astype(BF16))

    def xcopy(dx):
        xx = lax.rem(x + dx, NX)
        at = pl.multiple_of(16 * lax.rem(xx, 2), 16)
        return remote(
            flux.at[xx // 2, pl.ds(at, 48)], fx.at[x], x_send.at[dx], x_recv.at[x], band, xx
        )

    def xcopy_in(dx):
        xx = lax.rem(x + dx, NX)
        at = pl.multiple_of(16 * lax.rem(xx, 2), 16)
        return remote(
            flux.at[xx // 2, pl.ds(at, 48)], fx.at[xx], x_send.at[dx], x_recv.at[xx], band, xx
        )

    def acopy(k, d):
        idx = lax.rem(mine[k] + d, group)
        return remote(
            strips.at[k],
            gath.at[k, mine[k]],
            a_send.at[k, idx],
            a_recv.at[k, mine[k]],
            group_band(k, idx),
            x,
        )

    def acopy_in(k, d):
        idx = lax.rem(mine[k] + d, group)
        return remote(
            strips.at[k],
            gath.at[k, idx],
            a_send.at[k, idx],
            a_recv.at[k, idx],
            group_band(k, idx),
            x,
        )

    for k in range(2):

        @pl.loop(1, n)
        def _(d):
            p2_in(k, d).wait_recv()

        total = jnp.zeros((64, 192), F32)
        for t in range(n):
            total = total + part[k, t].astype(F32)
        tile_flux = (total * mask[k]).astype(BF16)
        flux[k] = tile_flux
        for f in range(3):
            stacked[f * 64 : f * 64 + 64, :] = tile_flux[:, f * 64 : f * 64 + 64]
        ns = mm(pick_rows, stacked[...])
        we = mm_nt(pick_cols, tile_flux)
        strips[k, 0:16, :] = jnp.concatenate([ns[0:16], we[0:16]], axis=1).astype(BF16)
        strips[k, 16:32, :] = jnp.concatenate([ns[16:32] + we[16:32], we[32:48]], axis=1).astype(
            BF16
        )

        @pl.loop(1, group)
        def _(d):
            acopy(k, d).start()

        gath[k, mine[k]] = strips[k]

    for dx in range(1, NX):
        xcopy(dx).start()
    fx[x] = flux[x // 2, pl.ds(pl.multiple_of(16 * h, 16), 48), :]

    def bcopy(k, t, xx):
        return remote(
            msgs.at[k, t, xx],
            rb.at[k, x, ring[k]],
            b_send.at[k, t, xx],
            b_recv.at[k, x, ring[k]],
            ring_band(k, t),
            xx,
        )

    def bcopy_in(k, t, xx):
        return remote(
            msgs.at[k, t, xx],
            rb.at[k, xx, t],
            b_send.at[k, t, xx],
            b_recv.at[k, xx, t],
            ring_band(k, t),
            xx,
        )

    def each_b(k, fn):
        @pl.loop(1, NX)
        def _(dx):
            fn(k, ring[k], lax.rem(x + dx, NX))

        @pl.loop(1, n)
        def _(d):
            for dx in range(NX):
                fn(k, lax.rem(ring[k] + d, n), lax.rem(x + dx, NX))

    low = iota((mrows, 128), 1) < 64
    body_rows = lax.rem(iota((mrows, 128), 0), 16) < 9
    for k in range(2):

        @pl.loop(1, group)
        def _(d):
            acopy_in(k, d).wait_recv()

        flat = gath[k].reshape(mcols, 128)
        msg = jnp.where(low & body_rows, mm(kmats[k, 0], flat), mm(kmats[k, 1], flat))
        msgs[k] = msg.astype(BF16).reshape(n, NX, 16, 128)
        each_b(k, lambda k, t, xx: bcopy(k, t, xx).start())
        rb[k, x, ring[k]] = msgs[k, ring[k], x]

    for dx in range(1, NX):
        xcopy_in(dx).wait_recv()
    for f in range(12):
        dmat[f * 48 : f * 48 + 48, 0:64] = fx[f // 3, :, (f % 3) * 64 : (f % 3) * 64 + 64]
    for k in range(2):
        each_b(k, lambda k, t, xx: bcopy_in(k, t, xx).wait_recv())
    total = jnp.zeros((NX, 16, 128), F32)
    for k in range(2):
        for t in range(n):
            total = total + rb[k, :, t].astype(F32)
    edge = total.reshape(64, 128)
    dmat[576:640, 0:64] = edge[:, 0:64].astype(BF16)
    elow = iota((64, 128), 1) < 64
    both = jnp.concatenate([jnp.where(elow, edge, 0.0), jnp.where(elow, 0.0, edge)], axis=0)
    picked = mm_nt(rowsel[0], both.astype(BF16)) * rowsel[1].astype(F32)
    yx[...] = (mm(smat[...], dmat[...]) + mm(picked.astype(BF16), collapse)).astype(BF16)
    pair_rows = jnp.concatenate([yx[0:592, :], yx[16:608, :]], axis=1)
    for b in range(7):
        zbuf[:, b] = (
            mm(pair_rows, shift_all[:, b * 128 : b * 128 + 128]).astype(BF16).reshape(37, 16, 128)
        )

    @pl.loop(0, 8)
    def _(i):
        left = zbuf[pl.ds(4 * i, 7)].reshape(wide, 128)
        right = zbuf[pl.ds(4 * i + 2, 7)].reshape(wide, 128)
        mixed = mm(c_all[...].reshape(192, wide), jnp.concatenate([left, right], axis=1))
        mean = jnp.sum(mixed, axis=0, keepdims=True) * (1.0 / 192.0)
        sq = jnp.sum(mixed * mixed, axis=0, keepdims=True) * (1.0 / 192.0)
        scale = lax.rsqrt(sq - mean * mean + 1e-06)
        normed = ((mixed - mean) * scale).astype(BF16)
        centre = jnp.concatenate([zbuf[4 * i + 3, 3], zbuf[4 * i + 5, 3]], axis=1)
        inner = mm(s_all[...].reshape(192, 16), centre).astype(BF16).astype(F32)
        hc = jnp.concatenate([hcol[...], hcol[...]], axis=1)
        acc = jnp.sum(inner * hc, axis=0, keepdims=True)
        for q in range(6):
            blk = slice(q * 128, q * 128 + 128)
            bias = jnp.concatenate([bcol[blk, :], bcol[blk, :]], axis=1)
            vals = jnp.concatenate([vcol[blk, :], vcol[blk, :]], axis=1)
            pre = mm(winp[blk, :], normed) + bias
            inside = pre * (0.7978845608 + (0.7978845608 * 0.044715) * (pre * pre))
            acc = acc + jnp.sum(vals * (pre * (1.0 + jnp.tanh(inside))), axis=0, keepdims=True)
        res[i] = acc

    out[x] = jnp.concatenate([res[i] for i in range(8)], axis=0)

    def fcopy(dx):
        xx = lax.rem(x + dx, NX)
        return remote(out.at[x], out.at[x], f_send.at[dx], f_recv.at[x], band, xx)

    def fcopy_in(dx):
        xx = lax.rem(x + dx, NX)
        return remote(out.at[x], out.at[xx], f_send.at[dx], f_recv.at[xx], band, xx)

    for dx in range(1, NX):
        fcopy(dx).start()

    for k in range(2):

        @pl.loop(1, group)
        def _(d):
            p1(k, d).wait_send()
            acopy(k, d).wait_send()

        @pl.loop(1, n)
        def _(d):
            p2(k, d).wait_send()

        each_b(k, lambda k, t, xx: bcopy(k, t, xx).wait_send())
    for dx in range(1, NX):
        xcopy(dx).wait_send()
        for i in range(5):
            share(i, dx).wait_send()
    for dx in range(1, NX):
        fcopy(dx).wait_send()
        fcopy_in(dx).wait_recv()


def body(
    side,
    atmos,
    remap_lat,
    remap_lon,
    pair_tile,
    pair_col,
    tile_owner,
    neighbours,
    land_mask,
    stem_w,
    dw_w,
    ln_gain,
    w_in,
    b_in,
    w_out,
    head_w,
):
    n = side
    group = n * CORES
    pairs = pair_col.shape[0]
    ints = jnp.concatenate(
        [tile_owner[None], pair_tile.T, pair_col[None], neighbours.T, tile_owner[None]], axis=0
    )
    atm = atmos.reshape(12, 45, 32).transpose(2, 0, 1)
    atm = jnp.pad(atm, ((0, 0), (0, 4), (0, 3))).reshape(512, 48)
    lat = remap_lat.transpose(2, 1, 0)
    lon = remap_lon.transpose(1, 2, 0)
    mask = jnp.tile(land_mask.reshape(2, 64, 64), (1, 1, 3)).astype(F32)
    small = jnp.stack(
        [jnp.pad(b_in, (0, 64)), jnp.pad(ln_gain, (0, 208)), jnp.pad(head_w, (0, 208))]
    )
    small = jnp.pad(small, ((0, 13), (0, 0)))
    vmem = pltpu.VMEM
    dma = pltpu.SemaphoreType.DMA
    frows = 38 * 16
    result = pl.pallas_call(
        functools.partial(kernel, n),
        out_shape=jax.ShapeDtypeStruct((NX, 8, 256), F32),
        in_specs=[pl.BlockSpec(memory_space=vmem)] * 10,
        out_specs=pl.BlockSpec(memory_space=vmem),
        scratch_shapes=[
            vmem((32, 16, pairs), F32),
            vmem((4, 256, pairs), BF16),
            vmem((2 * group, 4, 2 * n, 256), BF16),
            vmem((2, group, 4, 2 * n, 256), BF16),
            vmem((2, n, 64, 192), BF16),
            vmem((2, n, 64, 192), BF16),
            vmem((2, 64, 192), BF16),
            vmem((192, 64), BF16),
            vmem((2, 32, 128), BF16),
            vmem((2, group, 32, 128), BF16),
            vmem((2, 2, n * NX * 16, group * 32), BF16),
            vmem((2, n, NX, 16, 128), BF16),
            vmem((2, NX, n, 16, 128), BF16),
            vmem((NX, 48, 192), BF16),
            vmem((640, 128), BF16),
            vmem((frows, 640), BF16),
            vmem((2, frows, 128), BF16),
            vmem((frows, 128), BF16),
            vmem((37, 7, 16, 128), BF16),
            vmem((256, 896), BF16),
            vmem((NX, 192, 192), BF16),
            vmem((NX, 192, 192), BF16),
            vmem((48, 784), BF16),
            vmem((NX, 48, 784), BF16),
            vmem((48, 16), BF16),
            vmem((NX, 48, 16), BF16),
            vmem((NX, 16, 256), BF16),
            vmem((768, 192), BF16),
            vmem((768, 128), F32),
            vmem((768, 128), F32),
            vmem((192, 128), F32),
            vmem((8, 1, 256), F32),
            dma((2, group)),
            dma((2, group)),
            dma((2, n)),
            dma((2, n)),
            dma((2, group)),
            dma((2, group)),
            dma((NX,)),
            dma((NX,)),
            dma((2, n, NX)),
            dma((2, NX, n)),
            dma((5, NX)),
            dma((5, NX)),
            dma((NX,)),
            dma((NX,)),
            dma((1,)),
        ],
        compiler_params=pltpu.CompilerParams(
            collective_id=0, has_side_effects=True, vmem_limit_bytes=56 * 1024 * 1024
        ),
        cost_estimate=pl.CostEstimate(flops=4000000000, bytes_accessed=4000000, transcendentals=2000000),
    )(ints, atm, lat, lon, mask, stem_w, dw_w, small, w_in, w_out)
    return result.reshape(2, 4096) * land_mask.astype(F32)


def solution(mesh):
    side = 1
    while side * side * CORES < mesh.shape["band"]:
        side *= 2
    return jax.shard_map(
        functools.partial(body, side),
        mesh=mesh,
        in_specs=(
            P("chan", "band", None),
            P("band", None, None),
            P("band", None, None),
            P("band", None),
            P("band"),
            P(),
            P(),
            P("band", None),
            P(None, "chan"),
            P("chan", None),
            P("chan"),
            P("chan", None),
            P("chan"),
            P("chan", None),
            P("chan"),
        ),
        out_specs=P("band", None),
        check_vma=False,
    )
```

```python
import functools

import jax
import jax.numpy as jnp
from jax import lax
from jax.experimental import pallas as pl
from jax.experimental.pallas import tpu as pltpu
from jax.sharding import PartitionSpec as P

MESH = pl.DeviceIdType.MESH
F32 = jnp.float32
BF16 = jnp.bfloat16
NX = 4
CORES = 2


def iota(shape, axis):
    return lax.broadcasted_iota(jnp.int32, shape, axis)


def onehot(mask):
    return jnp.where(mask, 1.0, 0.0).astype(BF16)


def mm(a, b):
    return lax.dot_general(a, b, (((1,), (0,)), ((), ())), preferred_element_type=F32)


def mm_nt(a, b):
    return lax.dot_general(a, b, (((1,), (1,)), ((), ())), preferred_element_type=F32)


def mm_tn(a, b):
    return lax.dot_general(a, b, (((0,), (0,)), ((), ())), preferred_element_type=F32)


def third(v):
    return jnp.where(v >= 6, 2, jnp.where(v >= 3, 1, 0))


def kernel(
    side,
    owner_hbm,
    tile_hbm,
    col_hbm,
    near_hbm,
    atm_hbm,
    lon_hbm,
    lat_hbm,
    stem_hbm,
    dw_hbm,
    b_in_hbm,
    gain_hbm,
    head_hbm,
    w_in_hbm,
    w_out_hbm,
    mask_hbm,
    out,
    owner_ref,
    tile_ref,
    col_ref,
    near_ref,
    atm,
    lon,
    lat,
    stem_w,
    dw_w,
    b_in,
    ln_gain,
    head_w,
    w_in,
    w_out,
    mask_ref,
    in_sems,
    arow,
    ashift,
    small_f,
    small,
    mrows_ref,
    mask,
    got_out,
    xw,
    pls,
    send,
    recv,
    agg,
    part,
    flux,
    stacked,
    strips,
    gath,
    kmats,
    msgs,
    rb,
    fx,
    dmat,
    smat,
    rowsel,
    yx,
    zbuf,
    shift_all,
    w_all,
    o_all,
    c_loc,
    c_all,
    s_loc,
    s_all,
    sm_all,
    winp,
    bcol,
    vcol,
    hcol,
    res,
    p1_send,
    p1_recv,
    p2_send,
    p2_recv,
    a_send,
    a_recv,
    x_send,
    x_recv,
    b_send,
    b_recv,
    w_send,
    w_recv,
    f_send,
    f_recv,
    loc_sem,
):
    n = side
    group = n * CORES
    band = lax.axis_index("band")
    x = lax.axis_index("chan")
    y = band // group
    zc = lax.rem(band, group)
    z = zc // CORES
    c = lax.rem(zc, CORES)
    mine = (zc, y * CORES + c)
    ring = (y, z)

    def band_at(yy, zz, cc):
        return (yy * n + zz) * CORES + cc

    def group_band(k, idx):
        if k == 0:
            return y * group + idx
        return band_at(idx // CORES, z, lax.rem(idx, CORES))

    def ring_band(k, t):
        return band_at(t, z, c) if k == 0 else band_at(y, t, c)

    def remote(src, dst, ssem, rsem, tb, tx):
        return pltpu.make_async_remote_copy(
            src_ref=src,
            dst_ref=dst,
            send_sem=ssem,
            recv_sem=rsem,
            device_id={"band": tb, "chan": tx},
            device_id_type=MESH,
        )

    loads = [
        pltpu.make_async_copy(src, dst, in_sems.at[i])
        for i, (src, dst) in enumerate(
            (
                (owner_hbm, owner_ref),
                (tile_hbm, tile_ref),
                (col_hbm, col_ref),
                (near_hbm, near_ref),
                (atm_hbm, atm),
                (lon_hbm, lon),
                (lat_hbm, lat),
                (stem_hbm, stem_w),
                (dw_hbm, dw_w),
                (b_in_hbm, b_in),
                (gain_hbm, ln_gain),
                (head_hbm, head_w),
                (w_in_hbm, w_in),
                (w_out_hbm, w_out),
                (mask_hbm, mask_ref),
            )
        )
    ]
    for load in loads:
        load.start()

    barrier = pltpu.get_barrier_semaphore()

    def greet(tb, tx):
        pl.semaphore_signal(
            barrier, inc=1, device_id={"band": tb, "chan": tx}, device_id_type=MESH
        )

    @pl.loop(1, group)
    def _(d):
        greet(y * group + lax.rem(zc + d, group), x)

    @pl.loop(1, n)
    def _(d):
        yy = lax.rem(y + d, n)
        greet(band_at(yy, z, 0), x)
        greet(band_at(yy, z, 1), x)

    @pl.loop(1, NX)
    def _(dx):
        xx = lax.rem(x + dx, NX)
        greet(band, xx)

        @pl.loop(1, n)
        def _(d):
            greet(band_at(lax.rem(y + d, n), z, c), xx)
            greet(band_at(y, lax.rem(z + d, n), c), xx)

    pairs = lon.shape[2]
    tiles = pairs
    lons = atm.shape[2]
    padded = arow.shape[1]
    arow[...] = jnp.zeros(arow.shape, F32)
    for i in range(5):
        loads[i].wait()
    for f in range(3):
        arow[4 * f : 4 * f + 4, 0:lons] = atm[f].astype(F32)
    row = arow[...]
    for i in range(32):
        moved = row if i == 0 else pltpu.roll(row, padded - i, 1)
        ashift[16 * i : 16 * i + 16, :] = moved.astype(BF16)
    owner = owner_ref[...]
    tile = tile_ref[...]
    col = col_ref[...]
    at_col = onehot(iota((padded, pairs), 0) == col)
    xw[...] = mm(ashift[...], at_col).reshape(32, 16, pairs)
    loads[5].wait()
    loads[6].wait()

    half = min(128, pairs)
    for ph in range(pairs // half):
        for jb in range(2):

            def step(ci, accs):
                block = lon[ci, jb * 32 : jb * 32 + 32, ph * half : (ph + 1) * half].astype(F32)
                return tuple(
                    accs[fr] + xw[ci, fr : fr + 1, ph * half : (ph + 1) * half] * block
                    for fr in range(12)
                )

            accs = lax.fori_loop(
                0, 32, step, tuple(jnp.zeros((32, half), F32) for _ in range(12)), unroll=4
            )
            for f in range(3):
                for r in range(4):
                    pls[r, f * 64 + jb * 32 : f * 64 + jb * 32 + 32, ph * half : (ph + 1) * half] = (
                        accs[f * 4 + r].astype(BF16)
                    )
    for r in range(4):
        pls[r, 192:256, :] = lat[:, r, :]

    ti = iota((tiles, pairs), 0)
    named = onehot(ti == tile)
    owner16 = jnp.broadcast_to(owner, (16, tiles)).astype(F32).astype(BF16)
    place = mm(owner16, named)[0:1, :].astype(jnp.int32)
    same = mm_tn(named, named)
    earlier = iota((pairs, pairs), 0) < iota((pairs, pairs), 1)
    rank = jnp.sum(jnp.where(earlier, same, 0.0), axis=0, keepdims=True).astype(jnp.int32)
    kk = lax.rem(place, 2)
    to_band = place // 2
    to_y = to_band // group
    to_zc = lax.rem(to_band, group)
    to_z = to_zc // CORES
    to_c = lax.rem(to_zc, CORES)
    slot = jnp.where(
        kk == 0,
        (to_zc * n + to_y) * 2 + rank,
        ((group + to_y * CORES + to_c) * n + to_z) * 2 + rank,
    )
    slots = 2 * group * n * 2
    perm = onehot(iota((slots, pairs), 0) == slot)
    for r in range(4):
        send[:, r] = mm_nt(perm, pls[r]).astype(BF16).reshape(2 * group, 2 * n, 256)

    greetings = (group - 1) + 2 * (n - 1) + 3 * (2 * n - 1)
    pl.semaphore_wait(barrier, greetings)

    def p1(k, d):
        idx = lax.rem(mine[k] + d, group)
        return remote(
            send.at[k * group + idx],
            recv.at[k, mine[k]],
            p1_send.at[k, idx],
            p1_recv.at[k, mine[k]],
            group_band(k, idx),
            x,
        )

    def p1_in(k, d):
        idx = lax.rem(mine[k] + d, group)
        return remote(
            send.at[k * group + idx],
            recv.at[k, idx],
            p1_send.at[k, idx],
            p1_recv.at[k, idx],
            group_band(k, idx),
            x,
        )

    @pl.loop(1, group)
    def _(d):
        p1(0, d).start()
        p1(1, d).start()

    for k in range(2):
        recv[k, mine[k]] = send[k * group + mine[k]]

    for i in range(7, 15):
        loads[i].wait()
    small_f[...] = jnp.zeros(small_f.shape, F32)
    small_f[0:1, 0:192] = b_in[...].astype(F32)
    small_f[1:2, 0:48] = ln_gain[...].astype(F32)
    small_f[2:3, 0:48] = head_w[...].astype(F32)
    small[...] = small_f[...].astype(BF16)
    wide = 49 * 16
    lane = iota((49, wide), 1)
    spread = onehot(iota((49, wide), 0) == lane // 16)
    fields = onehot(iota((12, wide), 0) == lax.rem(iota((12, wide), 1), 16))
    combined = mm(dw_w[...], spread) * mm_tn(stem_w[...], fields)
    c_loc[...] = combined.astype(BF16)
    s_loc[...] = mm_tn(stem_w[...], onehot(iota((12, 16), 0) == iota((12, 16), 1))).astype(BF16)
    shares = ((w_in, w_all), (w_out, o_all), (c_loc, c_all), (s_loc, s_all), (small, sm_all))

    def share(i, dx):
        src, dst = shares[i]
        xx = lax.rem(x + dx, NX)
        return remote(src, dst.at[x], w_send.at[i, dx], w_recv.at[i, x], band, xx)

    def share_in(i, dx):
        src, dst = shares[i]
        xx = lax.rem(x + dx, NX)
        return remote(src, dst.at[xx], w_send.at[i, dx], w_recv.at[i, xx], band, xx)

    for dx in range(1, NX):
        for i in (4, 2, 3, 1, 0):
            share(i, dx).start()
    for src, dst in shares:
        dst[x] = src[...]

    ui = iota((tiles, tiles), 0)
    owner1 = jnp.broadcast_to(owner + 1, (16, tiles)).astype(F32).astype(BF16)
    near_rows = [mm(owner1, onehot(ui == near_ref[s : s + 1, :]))[0:1, :] for s in range(4)]
    near = jnp.concatenate(near_rows + [jnp.zeros((12, tiles), F32)], axis=0).astype(BF16)
    near_at = mm_nt(near, onehot(ui == owner)).astype(BF16)
    mrows = n * NX * 16
    mcols = group * 32
    mr = iota((mrows, tiles), 0)
    mt, mx, mrho = mr // 64, lax.rem(mr // 16, NX), lax.rem(mr, 16)
    ci = iota((mrows, mcols), 1)
    rho = lax.rem(iota((mrows, mcols), 0), 16)
    to_h = lax.rem(iota((mrows, mcols), 0) // 16, 2)
    src, src_half, src_rho = ci // 32, lax.rem(ci // 16, 2), lax.rem(ci, 16)
    for k in range(2):
        to_place = 2 * (ring_band(k, mt)) + mx // 2
        cols = mm_nt(onehot(iota((mrows, tiles), 1) == to_place), near_at).astype(jnp.int32)
        if k == 0:
            src_place = 2 * (y * group + src)
        else:
            src_place = 2 * band_at(src // CORES, z, lax.rem(src, CORES)) + 1
        src_tag = jnp.where(src_rho == rho, src_place + 1, -1)
        col_ns = jnp.where(to_h == 0, cols[:, 0:1], cols[:, 1:2])
        col_we = jnp.where(rho < 9, cols[:, 2:3], cols[:, 3:4])
        half_we = jnp.where(rho < 9, 0, 1)
        kmats[k, 0] = onehot((col_ns == src_tag) & (src_half == to_h))
        kmats[k, 1] = onehot((col_we == src_tag) & (src_half == half_we))

    for k in range(2):
        for i in range(32):
            mrows_ref[k, i : i + 1, :] = mask_ref[k : k + 1, 128 * i : 128 * i + 128].astype(F32)
        mpick = onehot(iota((64, 32), 1) == iota((64, 32), 0) // 2)
        mfull = mm(mpick, mrows_ref[k].astype(BF16))
        mswap = pltpu.roll(mfull, 64, 1)
        meven = lax.rem(iota((64, 128), 0), 2) * 64 + iota((64, 128), 1)
        keep = (meven < 64) | (meven >= 128)
        mask[k] = jnp.where(keep, mfull, mswap)

    h = lax.rem(x, 2)
    frows = 38 * 16
    fr_row = iota((frows, 640), 0)
    r_row, f_row = fr_row // 16, lax.rem(fr_row, 16)
    fx_row = f_row // 3
    fl_row = f_row - 3 * fx_row
    strip_a = jnp.where(h == 0, r_row, r_row - 35)
    in_strip = (strip_a >= 0) & (strip_a <= 2)
    want = jnp.where(
        in_strip,
        576 + fx_row * 16 + fl_row * 3 + strip_a,
        f_row * 48 + jnp.where(h == 0, r_row - 3, r_row + 13),
    )
    smat[...] = onehot((want == iota((frows, 640), 1)) & (f_row < 12))
    rr = iota((frows, 128), 0) // 16
    ff = lax.rem(iota((frows, 128), 0), 16)
    ll = iota((frows, 128), 1)
    cell = rr - 3 + 32 * h
    rowsel[0] = onehot((cell == lax.rem(ll, 64)) & (cell >= 0) & (cell < 64))
    lo = ll < 64
    lx, lrho = lax.rem(ll, 64) // 16, lax.rem(ll, 16)
    fa = jnp.where(lo, lrho - 9, jnp.where(lrho < 9, lrho, lrho - 2))
    ok = (lo & (lrho >= 9)) | (jnp.logical_not(lo) & (lrho < 11))
    rowsel[1] = onehot(ok & (3 * lx + third(fa) == ff))
    kr = iota((128, 128), 0)
    klo = kr < 64
    krho = lax.rem(kr, 16)
    kfa = jnp.where(klo, krho - 9, jnp.where(krho < 9, krho, krho - 2))
    kwest = jnp.logical_not(klo) & (krho < 9)
    lane_to = jnp.where(kwest, 64, 67) + kfa - 3 * third(kfa)
    collapse = onehot(lane_to == iota((128, 128), 1))
    ar = iota((256, 896), 0)
    al = lax.rem(ar, 128)
    ncol = jnp.where(al < 64, al + 3, jnp.where(al < 67, al - 64, jnp.where(al < 70, al, -999)))
    bc = iota((256, 896), 1)
    shift_all[...] = onehot(
        (ar // 128 == lax.rem(bc, 128) // 64) & (ncol == lax.rem(bc, 64) + bc // 128)
    )
    dmat[...] = jnp.zeros(dmat.shape, BF16)
    sr = iota((32, 192), 0)
    sl = iota((32, 192), 1)
    srho = lax.rem(sr, 16)
    sfl = third(srho)
    sa = srho - 3 * sfl
    pick_rows = onehot(
        (srho < 9) & (sl // 64 == sfl) & (lax.rem(sl, 64) == sa + jnp.where(sr < 16, 61, 0))
    )
    er = iota((48, 192), 0)
    el = iota((48, 192), 1)
    erho = lax.rem(er, 16)
    efa = jnp.where(er < 16, erho, jnp.where(er < 32, erho - 9, erho - 2))
    eok = (
        ((er < 16) & (erho < 9))
        | ((er >= 16) & (er < 32) & (erho >= 9))
        | ((er >= 32) & (erho >= 9) & (erho < 11))
    )
    efl = third(efa)
    ea = efa - 3 * efl + jnp.where(er < 16, 61, 0)
    pick_cols = onehot(eok & (el // 64 == efl) & (lax.rem(el, 64) == ea))

    def p2(k, d):
        t = lax.rem(ring[k] + d, n)
        return remote(
            agg.at[k, t],
            part.at[k, ring[k]],
            p2_send.at[k, t],
            p2_recv.at[k, ring[k]],
            ring_band(k, t),
            x,
        )

    def p2_in(k, d):
        t = lax.rem(ring[k] + d, n)
        return remote(
            agg.at[k, t],
            part.at[k, t],
            p2_send.at[k, t],
            p2_recv.at[k, t],
            ring_band(k, t),
            x,
        )

    krows = group * 8 * n
    k_tile = lax.rem(iota((64, krows), 1) // 2, n)
    for k in range(2):

        @pl.loop(1, group)
        def _(d):
            p1_in(k, d).wait_recv()

        got = recv[k].reshape(krows, 256)
        lat_t = got[:, 128:256].astype(F32).T[64:128, :]
        lhs = jnp.concatenate(
            [jnp.where(k_tile == t, lat_t, 0.0).astype(BF16) for t in range(n)], axis=0
        )
        sums = mm(lhs, got[:, 0:192])
        agg[k, :, 0:64, :] = sums[:, 0:128].astype(BF16).reshape(n, 64, 128)
        last = sums[:, 128:192].reshape(n, 2, 32, 64)
        agg[k, :, 64:96, :] = jnp.concatenate([last[:, 0], last[:, 1]], axis=2).astype(BF16)

        @pl.loop(1, n)
        def _(d):
            p2(k, d).start()

        part[k, ring[k]] = agg[k, ring[k]]

    def xcopy(dx):
        xx = lax.rem(x + dx, NX)
        at = pl.multiple_of(16 * lax.rem(xx, 2), 16)
        return remote(
            flux.at[xx // 2, pl.ds(at, 48)], fx.at[x], x_send.at[dx], x_recv.at[x], band, xx
        )

    def xcopy_in(dx):
        xx = lax.rem(x + dx, NX)
        at = pl.multiple_of(16 * lax.rem(xx, 2), 16)
        return remote(
            flux.at[xx // 2, pl.ds(at, 48)], fx.at[xx], x_send.at[dx], x_recv.at[xx], band, xx
        )

    def acopy(k, d):
        idx = lax.rem(mine[k] + d, group)
        return remote(
            strips.at[k],
            gath.at[k, mine[k]],
            a_send.at[k, idx],
            a_recv.at[k, mine[k]],
            group_band(k, idx),
            x,
        )

    def acopy_in(k, d):
        idx = lax.rem(mine[k] + d, group)
        return remote(
            strips.at[k],
            gath.at[k, idx],
            a_send.at[k, idx],
            a_recv.at[k, idx],
            group_band(k, idx),
            x,
        )

    for k in range(2):

        @pl.loop(1, n)
        def _(d):
            p2_in(k, d).wait_recv()

        total = part[k, 0].astype(F32)
        for t in range(1, n):
            total = total + part[k, t].astype(F32)
        last = jnp.concatenate([total[64:96, 0:64], total[64:96, 64:128]], axis=0)
        masked = [total[0:64, :] * mask[k], last * mask[k, :, 0:64]]
        tile_flux = jnp.concatenate(masked, axis=1).astype(BF16)
        flux[k] = tile_flux
        for f in range(3):
            stacked[f * 64 : f * 64 + 64, :] = tile_flux[:, f * 64 : f * 64 + 64]
        ns = mm(pick_rows, stacked[...])
        we = mm_nt(pick_cols, tile_flux)
        strips[k, 0:16, :] = jnp.concatenate([ns[0:16], we[0:16]], axis=1).astype(BF16)
        strips[k, 16:32, :] = jnp.concatenate([ns[16:32] + we[16:32], we[32:48]], axis=1).astype(
            BF16
        )

        @pl.loop(1, group)
        def _(d):
            acopy(k, d).start()

        gath[k, mine[k]] = strips[k]

    for dx in range(1, NX):
        xcopy(dx).start()
    fx[x] = flux[x // 2, pl.ds(pl.multiple_of(16 * h, 16), 48), :]

    def bcopy(k, t, xx):
        return remote(
            msgs.at[k, t, xx],
            rb.at[k, x, ring[k]],
            b_send.at[k, t, xx],
            b_recv.at[k, x, ring[k]],
            ring_band(k, t),
            xx,
        )

    def bcopy_in(k, t, xx):
        return remote(
            msgs.at[k, t, xx],
            rb.at[k, xx, t],
            b_send.at[k, t, xx],
            b_recv.at[k, xx, t],
            ring_band(k, t),
            xx,
        )

    def each_b(k, fn):
        @pl.loop(1, NX)
        def _(dx):
            fn(k, ring[k], lax.rem(x + dx, NX))

        @pl.loop(1, n)
        def _(d):
            for dx in range(NX):
                fn(k, lax.rem(ring[k] + d, n), lax.rem(x + dx, NX))

    low = iota((mrows, 128), 1) < 64
    body_rows = lax.rem(iota((mrows, 128), 0), 16) < 9
    for k in range(2):

        @pl.loop(1, group)
        def _(d):
            acopy_in(k, d).wait_recv()

        flat = gath[k].reshape(mcols, 128)
        msg = jnp.where(low & body_rows, mm(kmats[k, 0], flat), mm(kmats[k, 1], flat))
        msgs[k] = msg.astype(BF16).reshape(n, NX, 16, 128)
        each_b(k, lambda k, t, xx: bcopy(k, t, xx).start())
        rb[k, x, ring[k]] = msgs[k, ring[k], x]

    for dx in range(1, NX):
        for i in range(5):
            share_in(i, dx).wait_recv()
    gains = jnp.zeros((16, 192), F32)
    for i in range(NX):
        put = onehot(iota((256, 192), 1) == jnp.where(iota((256, 192), 0) < 48, iota((256, 192), 0) + 48 * i, -1))
        gains = gains + mm(sm_all[i], put)
    row2 = onehot(iota((16, 128), 0) == 2)
    row0 = onehot(iota((16, 128), 0) == 0)
    head = mm_tn(gains.astype(BF16), row2)
    hcol[...] = head
    for i in range(NX):
        blk = pl.ds(i * 192, 192)
        winp[blk, :] = (w_all[i].astype(F32) * gains[1:2, :]).astype(BF16)
        bcol[blk, :] = mm_tn(sm_all[i, :, 0:192], row0)
        vcol[blk, :] = 0.5 * mm(o_all[i], head.astype(BF16))

    for dx in range(1, NX):
        xcopy_in(dx).wait_recv()
    for f in range(12):
        dmat[f * 48 : f * 48 + 48, 0:64] = fx[f // 3, :, (f % 3) * 64 : (f % 3) * 64 + 64]
    for k in range(2):
        each_b(k, lambda k, t, xx: bcopy_in(k, t, xx).wait_recv())
    total = jnp.zeros((NX, 16, 128), F32)
    for k in range(2):
        for t in range(n):
            total = total + rb[k, :, t].astype(F32)
    edge = total.reshape(64, 128)
    dmat[576:640, 0:64] = edge[:, 0:64].astype(BF16)
    elow = iota((64, 128), 1) < 64
    both = jnp.concatenate([jnp.where(elow, edge, 0.0), jnp.where(elow, 0.0, edge)], axis=0)
    picked = mm_nt(rowsel[0], both.astype(BF16)) * rowsel[1].astype(F32)
    yx[...] = (mm(smat[...], dmat[...]) + mm(picked.astype(BF16), collapse)).astype(BF16)
    pair_rows = jnp.concatenate([yx[0:592, :], yx[16:608, :]], axis=1)
    for b in range(7):
        zbuf[:, b] = (
            mm(pair_rows, shift_all[:, b * 128 : b * 128 + 128]).astype(BF16).reshape(37, 16, 128)
        )

    @pl.loop(0, 8, unroll=2)
    def _(i):
        left = zbuf[pl.ds(4 * i, 7)].reshape(wide, 128)
        right = zbuf[pl.ds(4 * i + 2, 7)].reshape(wide, 128)
        mixed = mm(c_all[...].reshape(192, wide), jnp.concatenate([left, right], axis=1))
        mean = jnp.sum(mixed, axis=0, keepdims=True) * (1.0 / 192.0)
        sq = jnp.sum(mixed * mixed, axis=0, keepdims=True) * (1.0 / 192.0)
        scale = lax.rsqrt(sq - mean * mean + 1e-06)
        normed = ((mixed - mean) * scale).astype(BF16)
        centre = jnp.concatenate([zbuf[4 * i + 3, 3], zbuf[4 * i + 5, 3]], axis=1)
        inner = mm(s_all[...].reshape(192, 16), centre).astype(BF16).astype(F32)
        hc = jnp.concatenate([hcol[...], hcol[...]], axis=1)
        acc = jnp.sum(inner * hc, axis=0, keepdims=True)
        for q in range(6):
            blk = slice(q * 128, q * 128 + 128)
            bias = jnp.concatenate([bcol[blk, :], bcol[blk, :]], axis=1)
            vals = jnp.concatenate([vcol[blk, :], vcol[blk, :]], axis=1)
            pre = mm(winp[blk, :], normed) + bias
            inside = pre * (0.7978845608 + (0.7978845608 * 0.044715) * (pre * pre))
            acc = acc + jnp.sum(vals * (pre * (1.0 + jnp.tanh(inside))), axis=0, keepdims=True)
        res[i] = acc

    got_out[x] = jnp.concatenate([res[i] for i in range(8)], axis=0)

    def fcopy(dx):
        xx = lax.rem(x + dx, NX)
        return remote(got_out.at[x], got_out.at[x], f_send.at[dx], f_recv.at[x], band, xx)

    def fcopy_in(dx):
        xx = lax.rem(x + dx, NX)
        return remote(got_out.at[x], got_out.at[xx], f_send.at[dx], f_recv.at[xx], band, xx)

    for dx in range(1, NX):
        fcopy(dx).start()

    for k in range(2):

        @pl.loop(1, group)
        def _(d):
            p1(k, d).wait_send()
            acopy(k, d).wait_send()

        @pl.loop(1, n)
        def _(d):
            p2(k, d).wait_send()

        each_b(k, lambda k, t, xx: bcopy(k, t, xx).wait_send())
    for dx in range(1, NX):
        xcopy(dx).wait_send()
        for i in range(5):
            share(i, dx).wait_send()
    for dx in range(1, NX):
        fcopy(dx).wait_send()
        fcopy_in(dx).wait_recv()
    for k in range(2):
        for i in range(16):
            lanes = slice(256 * i, 256 * i + 256)
            out[k : k + 1, lanes] = got_out[2 * k + i // 8, i % 8 : i % 8 + 1, :] * mask_ref[
                k : k + 1, lanes
            ].astype(F32)


def body(
    side,
    atmos,
    remap_lat,
    remap_lon,
    pair_tile,
    pair_col,
    tile_owner,
    neighbours,
    land_mask,
    stem_w,
    dw_w,
    ln_gain,
    w_in,
    b_in,
    w_out,
    head_w,
):
    n = side
    group = n * CORES
    pairs = pair_col.shape[0]
    operands = (
        tile_owner[None],
        pair_tile.T,
        pair_col[None],
        neighbours.T,
        atmos,
        remap_lon.transpose(1, 2, 0),
        remap_lat.transpose(1, 2, 0),
        stem_w,
        dw_w,
        b_in[None],
        ln_gain[None],
        head_w[None],
        w_in,
        w_out,
        land_mask,
    )
    vmem = pltpu.VMEM
    dma = pltpu.SemaphoreType.DMA
    frows = 38 * 16
    return pl.pallas_call(
        functools.partial(kernel, n),
        out_shape=jax.ShapeDtypeStruct((2, 4096), F32),
        in_specs=[pl.BlockSpec(memory_space=pl.ANY)] * 15,
        out_specs=pl.BlockSpec(memory_space=vmem),
        scratch_shapes=[vmem(a.shape, a.dtype) for a in operands]
        + [
            dma((15,)),
            vmem((16, 1536), F32),
            vmem((512, 1536), BF16),
            vmem((16, 256), F32),
            vmem((16, 256), BF16),
            vmem((2, 32, 128), F32),
            vmem((2, 64, 128), F32),
            vmem((NX, 8, 256), F32),
            vmem((32, 16, pairs), F32),
            vmem((4, 256, pairs), BF16),
            vmem((2 * group, 4, 2 * n, 256), BF16),
            vmem((2, group, 4, 2 * n, 256), BF16),
            vmem((2, n, 96, 128), BF16),
            vmem((2, n, 96, 128), BF16),
            vmem((2, 64, 192), BF16),
            vmem((192, 64), BF16),
            vmem((2, 32, 128), BF16),
            vmem((2, group, 32, 128), BF16),
            vmem((2, 2, n * NX * 16, group * 32), BF16),
            vmem((2, n, NX, 16, 128), BF16),
            vmem((2, NX, n, 16, 128), BF16),
            vmem((NX, 48, 192), BF16),
            vmem((640, 128), BF16),
            vmem((frows, 640), BF16),
            vmem((2, frows, 128), BF16),
            vmem((frows, 128), BF16),
            vmem((37, 7, 16, 128), BF16),
            vmem((256, 896), BF16),
            vmem((NX, 192, 192), BF16),
            vmem((NX, 192, 192), BF16),
            vmem((48, 784), BF16),
            vmem((NX, 48, 784), BF16),
            vmem((48, 16), BF16),
            vmem((NX, 48, 16), BF16),
            vmem((NX, 16, 256), BF16),
            vmem((768, 192), BF16),
            vmem((768, 128), F32),
            vmem((768, 128), F32),
            vmem((192, 128), F32),
            vmem((8, 1, 256), F32),
            dma((2, group)),
            dma((2, group)),
            dma((2, n)),
            dma((2, n)),
            dma((2, group)),
            dma((2, group)),
            dma((NX,)),
            dma((NX,)),
            dma((2, n, NX)),
            dma((2, NX, n)),
            dma((5, NX)),
            dma((5, NX)),
            dma((NX,)),
            dma((NX,)),
            dma((1,)),
        ],
        compiler_params=pltpu.CompilerParams(
            collective_id=0, has_side_effects=True, vmem_limit_bytes=56 * 1024 * 1024
        ),
        cost_estimate=pl.CostEstimate(flops=4000000000, bytes_accessed=4000000, transcendentals=2000000),
    )(*operands)


def solution(mesh):
    side = 1
    while side * side * CORES < mesh.shape["band"]:
        side *= 2
    return jax.shard_map(
        functools.partial(body, side),
        mesh=mesh,
        in_specs=(
            P("chan", "band", None),
            P("band", None, None),
            P("band", None, None),
            P("band", None),
            P("band"),
            P(),
            P(),
            P("band", None),
            P(None, "chan"),
            P("chan", None),
            P("chan"),
            P("chan", None),
            P("chan"),
            P("chan", None),
            P("chan"),
        ),
        out_specs=P("band", None),
        check_vma=False,
    )
```

```python
import functools

import jax
import jax.numpy as jnp
from jax import lax
from jax.experimental import pallas as pl
from jax.experimental.pallas import tpu as pltpu
from jax.sharding import PartitionSpec as P

MESH = pl.DeviceIdType.MESH
F32 = jnp.float32
BF16 = jnp.bfloat16
NX = 4
CORES = 2


def iota(shape, axis):
    return lax.broadcasted_iota(jnp.int32, shape, axis)


def onehot(mask):
    return jnp.where(mask, 1.0, 0.0).astype(BF16)


def mm(a, b):
    return lax.dot_general(a, b, (((1,), (0,)), ((), ())), preferred_element_type=F32)


def mm_nt(a, b):
    return lax.dot_general(a, b, (((1,), (1,)), ((), ())), preferred_element_type=F32)


def mm_tn(a, b):
    return lax.dot_general(a, b, (((0,), (0,)), ((), ())), preferred_element_type=F32)


def sdiv(a, b):
    return lax.div(a, jnp.int32(b))


def third(v):
    return jnp.where(v >= 6, 2, jnp.where(v >= 3, 1, 0))


def kernel(
    side,
    owner_hbm,
    tile_hbm,
    col_hbm,
    near_hbm,
    atm_hbm,
    lon_hbm,
    lat_hbm,
    stem_hbm,
    dw_hbm,
    b_in_hbm,
    gain_hbm,
    head_hbm,
    w_in_hbm,
    w_out_hbm,
    mask_hbm,
    out,
    owner_ref,
    tile_ref,
    col_ref,
    near_ref,
    atm,
    lon,
    lat,
    stem_w,
    dw_w,
    b_in,
    ln_gain,
    head_w,
    w_in,
    w_out,
    mask_ref,
    in_sems,
    arow,
    ashift,
    small_f,
    small,
    mrows_ref,
    mask,
    got_out,
    xw,
    pls,
    send,
    recv,
    agg,
    part,
    flux,
    stacked,
    strips,
    gath,
    kmats,
    msgs,
    rb,
    edge_sel,
    fx,
    dmat,
    smat,
    rowsel,
    yx,
    zbuf,
    shift_all,
    w_all,
    o_all,
    c_loc,
    c_all,
    s_loc,
    s_all,
    sm_all,
    winp,
    bcol,
    vcol,
    hcol,
    res,
    p1_send,
    p1_recv,
    p2_send,
    p2_recv,
    a_send,
    a_recv,
    x_send,
    x_recv,
    b_send,
    b_recv,
    w_send,
    w_recv,
    f_send,
    f_recv,
):
    n = side
    group = n * CORES
    band = lax.axis_index("band")
    x = lax.axis_index("chan")
    y = sdiv(band, group)
    zc = lax.rem(band, group)
    z = sdiv(zc, CORES)
    c = lax.rem(zc, CORES)
    mine = (zc, y * CORES + c)
    ring = (y, z)

    def band_at(yy, zz, cc):
        return (yy * n + zz) * CORES + cc

    def group_band(k, idx):
        if k == 0:
            return y * group + idx
        return band_at(sdiv(idx, CORES), z, lax.rem(idx, CORES))

    def ring_band(k, t):
        return band_at(t, z, c) if k == 0 else band_at(y, t, c)

    def remote(src, dst, ssem, rsem, tb, tx):
        return pltpu.make_async_remote_copy(
            src_ref=src,
            dst_ref=dst,
            send_sem=ssem,
            recv_sem=rsem,
            device_id={"band": tb, "chan": tx},
            device_id_type=MESH,
        )

    def settle(ref, sem):
        pltpu.make_async_copy(ref, ref, sem).wait()

    loads = [
        pltpu.make_async_copy(src, dst, in_sems.at[i])
        for i, (src, dst) in enumerate(
            (
                (owner_hbm, owner_ref),
                (tile_hbm, tile_ref),
                (col_hbm, col_ref),
                (near_hbm, near_ref),
                (atm_hbm, atm),
                (lon_hbm, lon),
                (lat_hbm, lat),
                (stem_hbm, stem_w),
                (dw_hbm, dw_w),
                (b_in_hbm, b_in),
                (gain_hbm, ln_gain),
                (head_hbm, head_w),
                (w_in_hbm, w_in),
                (w_out_hbm, w_out),
                (mask_hbm, mask_ref),
            )
        )
    ]
    for load in loads:
        load.start()

    barrier = pltpu.get_barrier_semaphore()

    def greet(tb, tx):
        pl.semaphore_signal(
            barrier, inc=1, device_id={"band": tb, "chan": tx}, device_id_type=MESH
        )

    @pl.loop(1, group)
    def _(d):
        greet(y * group + lax.rem(zc + d, group), x)

    @pl.loop(1, n)
    def _(d):
        yy = lax.rem(y + d, n)
        greet(band_at(yy, z, 0), x)
        greet(band_at(yy, z, 1), x)

    @pl.loop(1, NX)
    def _(dx):
        xx = lax.rem(x + dx, NX)
        greet(band, xx)

        @pl.loop(1, n)
        def _(d):
            greet(band_at(lax.rem(y + d, n), z, c), xx)
            greet(band_at(y, lax.rem(z + d, n), c), xx)

    pairs = lon.shape[2]
    tiles = pairs
    lons = atm.shape[2]
    padded = arow.shape[1]
    arow[...] = jnp.zeros(arow.shape, F32)
    for i in range(5):
        loads[i].wait()
    for f in range(3):
        arow[4 * f : 4 * f + 4, 0:lons] = atm[f].astype(F32)
    row = arow[...]
    for i in range(32):
        moved = row if i == 0 else pltpu.roll(row, padded - i, 1)
        ashift[16 * i : 16 * i + 16, :] = moved.astype(BF16)
    owner = owner_ref[...]
    tile = tile_ref[...]
    col = col_ref[...]
    at_col = onehot(iota((padded, pairs), 0) == col)
    xw[...] = mm(ashift[...], at_col).reshape(32, 16, pairs)
    loads[5].wait()
    loads[6].wait()

    half = min(128, pairs)
    for ph in range(pairs // half):
        for jb in range(2):

            def step(ci, accs):
                block = lon[ci, jb * 32 : jb * 32 + 32, ph * half : (ph + 1) * half].astype(F32)
                return tuple(
                    accs[fr] + xw[ci, fr : fr + 1, ph * half : (ph + 1) * half] * block
                    for fr in range(12)
                )

            accs = lax.fori_loop(
                0, 32, step, tuple(jnp.zeros((32, half), F32) for _ in range(12)), unroll=4
            )
            for f in range(3):
                for r in range(4):
                    pls[r, f * 64 + jb * 32 : f * 64 + jb * 32 + 32, ph * half : (ph + 1) * half] = (
                        accs[f * 4 + r].astype(BF16)
                    )
    for r in range(4):
        pls[r, 192:256, :] = lat[:, r, :]

    ti = iota((tiles, pairs), 0)
    named = onehot(ti == tile)
    owner16 = jnp.broadcast_to(owner, (16, tiles)).astype(F32).astype(BF16)
    place = mm(owner16, named)[0:1, :].astype(jnp.int32)
    same = mm_tn(named, named)
    earlier = iota((pairs, pairs), 0) < iota((pairs, pairs), 1)
    rank = jnp.sum(jnp.where(earlier, same, 0.0), axis=0, keepdims=True).astype(jnp.int32)
    kk = lax.rem(place, 2)
    to_band = place // 2
    to_y = to_band // group
    to_zc = lax.rem(to_band, group)
    to_z = to_zc // CORES
    to_c = lax.rem(to_zc, CORES)
    slot = jnp.where(
        kk == 0,
        (to_zc * n + to_y) * 2 + rank,
        ((group + to_y * CORES + to_c) * n + to_z) * 2 + rank,
    )
    slots = 2 * group * n * 2
    perm = onehot(iota((slots, pairs), 0) == slot)
    for r in range(4):
        send[:, r] = mm_nt(perm, pls[r]).astype(BF16).reshape(2 * group, 2 * n, 256)

    greetings = (group - 1) + 2 * (n - 1) + 3 * (2 * n - 1)
    pl.semaphore_wait(barrier, greetings)

    def p1(k, d):
        idx = lax.rem(mine[k] + d, group)
        return remote(
            send.at[k * group + idx],
            recv.at[k, mine[k]],
            p1_send.at[k],
            p1_recv.at[k],
            group_band(k, idx),
            x,
        )

    @pl.loop(1, group)
    def _(d):
        p1(0, d).start()
        p1(1, d).start()

    for k in range(2):
        recv[k, mine[k]] = send[k * group + mine[k]]

    for i in range(7, 15):
        loads[i].wait()
    small_f[...] = jnp.zeros(small_f.shape, F32)
    small_f[0:1, 0:192] = b_in[...].astype(F32).reshape(1, 192)
    small_f[1:2, 0:48] = ln_gain[...].astype(F32)
    small_f[2:3, 0:48] = head_w[...].astype(F32)
    small[...] = small_f[...].astype(BF16)
    wide = 49 * 16
    lane = iota((49, wide), 1)
    spread = onehot(iota((49, wide), 0) == lane // 16)
    fields = onehot(iota((12, wide), 0) == lax.rem(iota((12, wide), 1), 16))
    combined = mm(dw_w[...], spread) * mm_tn(stem_w[...], fields)
    c_loc[...] = combined.astype(BF16)
    s_loc[...] = mm_tn(stem_w[...], onehot(iota((12, 16), 0) == iota((12, 16), 1))).astype(BF16)
    shares = ((w_in, w_all), (w_out, o_all), (c_loc, c_all), (s_loc, s_all), (small, sm_all))

    def share(i, dx):
        src, dst = shares[i]
        xx = lax.rem(x + dx, NX)
        return remote(src, dst.at[x], w_send.at[i], w_recv.at[i], band, xx)

    for dx in range(1, NX):
        for i in (4, 2, 3, 1, 0):
            share(i, dx).start()
    for src, dst in shares:
        dst[x] = src[...]

    ui = iota((tiles, tiles), 0)
    owner1 = jnp.broadcast_to(owner + 1, (16, tiles)).astype(F32).astype(BF16)
    near_rows = [mm(owner1, onehot(ui == near_ref[s : s + 1, :]))[0:1, :] for s in range(4)]
    near = jnp.concatenate(near_rows + [jnp.zeros((12, tiles), F32)], axis=0).astype(BF16)
    near_at = mm_nt(near, onehot(ui == owner)).astype(BF16)
    mrows = n * NX * 16
    mcols = group * 32
    mr = iota((mrows, tiles), 0)
    mt, mx, mrho = mr // 64, lax.rem(mr // 16, NX), lax.rem(mr, 16)
    ci = iota((mrows, mcols), 1)
    rho = lax.rem(iota((mrows, mcols), 0), 16)
    to_h = lax.rem(iota((mrows, mcols), 0) // 16, 2)
    src, src_half, src_rho = ci // 32, lax.rem(ci // 16, 2), lax.rem(ci, 16)
    for k in range(2):
        to_place = 2 * (ring_band(k, mt)) + mx // 2
        cols = mm_nt(onehot(iota((mrows, tiles), 1) == to_place), near_at).astype(jnp.int32)
        if k == 0:
            src_place = 2 * (y * group + src)
        else:
            src_place = 2 * band_at(src // CORES, z, lax.rem(src, CORES)) + 1
        src_tag = jnp.where(src_rho == rho, src_place + 1, -1)
        col_ns = jnp.where(to_h == 0, cols[:, 0:1], cols[:, 1:2])
        col_we = jnp.where(rho < 9, cols[:, 2:3], cols[:, 3:4])
        half_we = jnp.where(rho < 9, 0, 1)
        kmats[k, 0] = onehot((col_ns == src_tag) & (src_half == to_h))
        kmats[k, 1] = onehot((col_we == src_tag) & (src_half == half_we))

    for k in range(2):
        for i in range(32):
            mrows_ref[k, i : i + 1, :] = mask_ref[k : k + 1, 128 * i : 128 * i + 128].astype(F32)
        mpick = onehot(iota((64, 32), 1) == iota((64, 32), 0) // 2)
        mfull = mm(mpick, mrows_ref[k].astype(BF16))
        mswap = pltpu.roll(mfull, 64, 1)
        meven = lax.rem(iota((64, 128), 0), 2) * 64 + iota((64, 128), 1)
        keep = (meven < 64) | (meven >= 128)
        mask[k] = jnp.where(keep, mfull, mswap)

    h = lax.rem(x, 2)
    frows = 38 * 16
    fr_row = iota((frows, 640), 0)
    r_row, f_row = fr_row // 16, lax.rem(fr_row, 16)
    fx_row = f_row // 3
    fl_row = f_row - 3 * fx_row
    strip_a = jnp.where(h == 0, r_row, r_row - 35)
    in_strip = (strip_a >= 0) & (strip_a <= 2)
    want = jnp.where(
        in_strip,
        576 + fx_row * 16 + fl_row * 3 + strip_a,
        f_row * 48 + jnp.where(h == 0, r_row - 3, r_row + 13),
    )
    smat[...] = onehot((want == iota((frows, 640), 1)) & (f_row < 12) & (want < 576))
    er_row, er_f = iota((frows, 64), 0) // 16, lax.rem(iota((frows, 64), 0), 16)
    er_a = jnp.where(h == 0, er_row, er_row - 35)
    er_to = er_f // 3 * 16 + lax.rem(er_f, 3) * 3 + er_a
    edge_sel[...] = onehot(
        (er_to == iota((frows, 64), 1)) & (er_f < 12) & (er_a >= 0) & (er_a <= 2)
    )
    rr = iota((frows, 128), 0) // 16
    ff = lax.rem(iota((frows, 128), 0), 16)
    ll = iota((frows, 128), 1)
    cell = rr - 3 + 32 * h
    rowsel[0] = onehot((cell == lax.rem(ll, 64)) & (cell >= 0) & (cell < 64))
    lo = ll < 64
    lx, lrho = lax.rem(ll, 64) // 16, lax.rem(ll, 16)
    fa = jnp.where(lo, lrho - 9, jnp.where(lrho < 9, lrho, lrho - 2))
    ok = (lo & (lrho >= 9)) | (jnp.logical_not(lo) & (lrho < 11))
    rowsel[1] = onehot(ok & (3 * lx + third(fa) == ff))
    kr = iota((128, 128), 0)
    klo = kr < 64
    krho = lax.rem(kr, 16)
    kfa = jnp.where(klo, krho - 9, jnp.where(krho < 9, krho, krho - 2))
    kwest = jnp.logical_not(klo) & (krho < 9)
    lane_to = jnp.where(kwest, 64, 67) + kfa - 3 * third(kfa)
    collapse = onehot(lane_to == iota((128, 128), 1))
    ar = iota((256, 896), 0)
    al = lax.rem(ar, 128)
    ncol = jnp.where(al < 64, al + 3, jnp.where(al < 67, al - 64, jnp.where(al < 70, al, -999)))
    bc = iota((256, 896), 1)
    shift_all[...] = onehot(
        (ar // 128 == lax.rem(bc, 128) // 64) & (ncol == lax.rem(bc, 64) + bc // 128)
    )
    dmat[...] = jnp.zeros(dmat.shape, BF16)
    sr = iota((32, 192), 0)
    sl = iota((32, 192), 1)
    srho = lax.rem(sr, 16)
    sfl = third(srho)
    sa = srho - 3 * sfl
    pick_rows = onehot(
        (srho < 9) & (sl // 64 == sfl) & (lax.rem(sl, 64) == sa + jnp.where(sr < 16, 61, 0))
    )
    er = iota((48, 192), 0)
    el = iota((48, 192), 1)
    erho = lax.rem(er, 16)
    efa = jnp.where(er < 16, erho, jnp.where(er < 32, erho - 9, erho - 2))
    eok = (
        ((er < 16) & (erho < 9))
        | ((er >= 16) & (er < 32) & (erho >= 9))
        | ((er >= 32) & (erho >= 9) & (erho < 11))
    )
    efl = third(efa)
    ea = efa - 3 * efl + jnp.where(er < 16, 61, 0)
    pick_cols = onehot(eok & (el // 64 == efl) & (lax.rem(el, 64) == ea))

    def p2(k, d):
        t = lax.rem(ring[k] + d, n)
        return remote(
            agg.at[k, t],
            part.at[k, ring[k]],
            p2_send.at[k],
            p2_recv.at[k],
            ring_band(k, t),
            x,
        )

    krows = group * 8 * n
    k_tile = lax.rem(iota((64, krows), 1) // 2, n)
    for k in range(2):

        settle(recv.at[k, pl.ds(0, group - 1)], p1_recv.at[k])

        got = recv[k].reshape(krows, 256)
        lat_t = got[:, 128:256].astype(F32).T[64:128, :]
        lhs = jnp.concatenate(
            [jnp.where(k_tile == t, lat_t, 0.0).astype(BF16) for t in range(n)], axis=0
        )
        sums = mm(lhs, got[:, 0:192])
        agg[k, :, 0:64, :] = sums[:, 0:128].astype(BF16).reshape(n, 64, 128)
        last = sums[:, 128:192].reshape(n, 2, 32, 64)
        agg[k, :, 64:96, :] = jnp.concatenate([last[:, 0], last[:, 1]], axis=2).astype(BF16)

        @pl.loop(1, n)
        def _(d):
            p2(k, d).start()

        part[k, ring[k]] = agg[k, ring[k]]

    def xcopy(dx):
        xx = lax.rem(x + dx, NX)
        at = pl.multiple_of(16 * lax.rem(xx, 2), 16)
        return remote(
            flux.at[sdiv(xx, 2), pl.ds(at, 48)], fx.at[x], x_send.at[0], x_recv.at[0], band, xx
        )

    def acopy(k, d):
        idx = lax.rem(mine[k] + d, group)
        return remote(
            strips.at[k],
            gath.at[k, mine[k]],
            a_send.at[k],
            a_recv.at[k],
            group_band(k, idx),
            x,
        )

    for k in range(2):

        settle(part.at[k, pl.ds(0, n - 1)], p2_recv.at[k])

        total = part[k, 0].astype(F32)
        for t in range(1, n):
            total = total + part[k, t].astype(F32)
        last = jnp.concatenate([total[64:96, 0:64], total[64:96, 64:128]], axis=0)
        masked = [total[0:64, :] * mask[k], last * mask[k, :, 0:64]]
        tile_flux = jnp.concatenate(masked, axis=1).astype(BF16)
        flux[k] = tile_flux
        for f in range(3):
            stacked[f * 64 : f * 64 + 64, :] = tile_flux[:, f * 64 : f * 64 + 64]
        ns = mm(pick_rows, stacked[...])
        we = mm_nt(pick_cols, tile_flux)
        strips[k, 0:16, :] = jnp.concatenate([ns[0:16], we[0:16]], axis=1).astype(BF16)
        strips[k, 16:32, :] = jnp.concatenate([ns[16:32] + we[16:32], we[32:48]], axis=1).astype(
            BF16
        )

        @pl.loop(1, group)
        def _(d):
            acopy(k, d).start()

        gath[k, mine[k]] = strips[k]

    for dx in range(1, NX):
        xcopy(dx).start()
    fx[x] = flux[sdiv(x, 2), pl.ds(pl.multiple_of(16 * h, 16), 48), :]

    def bcopy(k, t, xx):
        return remote(
            msgs.at[k, t, xx],
            rb.at[k, x * n + ring[k]],
            b_send.at[k],
            b_recv.at[k],
            ring_band(k, t),
            xx,
        )

    def each_b(k, fn):
        @pl.loop(1, NX)
        def _(dx):
            fn(k, ring[k], lax.rem(x + dx, NX))

        @pl.loop(1, n)
        def _(d):
            for dx in range(NX):
                fn(k, lax.rem(ring[k] + d, n), lax.rem(x + dx, NX))

    low = iota((mrows, 128), 1) < 64
    body_rows = lax.rem(iota((mrows, 128), 0), 16) < 9
    for k in range(2):

        settle(gath.at[k, pl.ds(0, group - 1)], a_recv.at[k])

        flat = gath[k].reshape(mcols, 128)
        msg = jnp.where(low & body_rows, mm(kmats[k, 0], flat), mm(kmats[k, 1], flat))
        msgs[k] = msg.astype(BF16).reshape(n, NX, 16, 128)
        each_b(k, lambda k, t, xx: bcopy(k, t, xx).start())
        rb[k, x * n + ring[k]] = msgs[k, ring[k], x]

    for i, (_, dst) in enumerate(shares):
        settle(dst.at[pl.ds(0, NX - 1)], w_recv.at[i])
    gains = jnp.zeros((16, 192), F32)
    for i in range(NX):
        put = onehot(iota((256, 192), 1) == jnp.where(iota((256, 192), 0) < 48, iota((256, 192), 0) + 48 * i, -1))
        gains = gains + mm(sm_all[i], put)
    row2 = onehot(iota((16, 128), 0) == 2)
    row0 = onehot(iota((16, 128), 0) == 0)
    head = mm_tn(gains.astype(BF16), row2)
    hcol[...] = head
    for i in range(NX):
        blk = pl.ds(i * 192, 192)
        winp[blk, :] = (w_all[i].astype(F32) * gains[1:2, :]).astype(BF16)
        bcol[blk, :] = mm_tn(sm_all[i, :, 0:192], row0)
        vcol[blk, :] = 0.5 * mm(o_all[i], head.astype(BF16))

    settle(fx.at[pl.ds(0, NX - 1)], x_recv.at[0])
    for f in range(12):
        dmat[f * 48 : f * 48 + 48, 0:64] = fx[f // 3, :, (f % 3) * 64 : (f % 3) * 64 + 64]
    yx[...] = mm(smat[...], dmat[...]).astype(BF16)
    for k in range(2):
        settle(rb.at[k, pl.ds(0, NX * n - 1)], b_recv.at[k])
    total = jnp.zeros((NX, 16, 128), F32)
    for k in range(2):
        arrived = rb[k].reshape(NX, n, 16, 128)
        for t in range(n):
            total = total + arrived[:, t].astype(F32)
    edge = total.reshape(64, 128)
    elow = iota((64, 128), 1) < 64
    edge_low = jnp.where(elow, edge, 0.0)
    both = jnp.concatenate([edge_low, jnp.where(elow, 0.0, edge)], axis=0)
    picked = mm_nt(rowsel[0], both.astype(BF16)) * rowsel[1].astype(F32)
    outer_rows = mm(edge_sel[...], edge_low.astype(BF16)) + mm(picked.astype(BF16), collapse)
    yx[...] = (yx[...].astype(F32) + outer_rows).astype(BF16)
    pair_rows = jnp.concatenate([yx[0:592, :], yx[16:608, :]], axis=1)
    for b in range(7):
        zbuf[:, b] = (
            mm(pair_rows, shift_all[:, b * 128 : b * 128 + 128]).astype(BF16).reshape(37, 16, 128)
        )

    @pl.loop(0, 8, unroll=2)
    def _(i):
        left = zbuf[pl.ds(4 * i, 7)].reshape(wide, 128)
        right = zbuf[pl.ds(4 * i + 2, 7)].reshape(wide, 128)
        mixed = mm(c_all[...].reshape(192, wide), jnp.concatenate([left, right], axis=1))
        mean = jnp.sum(mixed, axis=0, keepdims=True) * (1.0 / 192.0)
        sq = jnp.sum(mixed * mixed, axis=0, keepdims=True) * (1.0 / 192.0)
        scale = lax.rsqrt(sq - mean * mean + 1e-06)
        normed = ((mixed - mean) * scale).astype(BF16)
        centre = jnp.concatenate([zbuf[4 * i + 3, 3], zbuf[4 * i + 5, 3]], axis=1)
        inner = mm(s_all[...].reshape(192, 16), centre).astype(BF16).astype(F32)
        hc = jnp.concatenate([hcol[...], hcol[...]], axis=1)
        acc = jnp.sum(inner * hc, axis=0, keepdims=True)
        for q in range(6):
            blk = slice(q * 128, q * 128 + 128)
            bias = jnp.concatenate([bcol[blk, :], bcol[blk, :]], axis=1)
            vals = jnp.concatenate([vcol[blk, :], vcol[blk, :]], axis=1)
            pre = mm(winp[blk, :], normed) + bias
            inside = pre * (0.7978845608 + (0.7978845608 * 0.044715) * (pre * pre))
            acc = acc + jnp.sum(vals * (pre * (1.0 + jnp.tanh(inside))), axis=0, keepdims=True)
        res[i] = acc

    got_out[x] = jnp.concatenate([res[i] for i in range(8)], axis=0)

    def fcopy(dx):
        xx = lax.rem(x + dx, NX)
        return remote(got_out.at[x], got_out.at[x], f_send.at[0], f_recv.at[0], band, xx)

    for dx in range(1, NX):
        fcopy(dx).start()

    for k in range(2):
        settle(send.at[pl.ds(0, group - 1)], p1_send.at[k])
        settle(part.at[k, pl.ds(0, n - 1)], p2_send.at[k])
        settle(gath.at[k, pl.ds(0, group - 1)], a_send.at[k])
        settle(rb.at[k, pl.ds(0, NX * n - 1)], b_send.at[k])
    settle(fx.at[pl.ds(0, NX - 1)], x_send.at[0])
    for i, (_, dst) in enumerate(shares):
        settle(dst.at[pl.ds(0, NX - 1)], w_send.at[i])
    settle(got_out.at[pl.ds(0, NX - 1)], f_send.at[0])
    settle(got_out.at[pl.ds(0, NX - 1)], f_recv.at[0])
    for k in range(2):
        for i in range(16):
            lanes = slice(256 * i, 256 * i + 256)
            out[k : k + 1, lanes] = got_out[2 * k + i // 8, i % 8 : i % 8 + 1, :] * mask_ref[
                k : k + 1, lanes
            ].astype(F32)


def body(
    side,
    atmos,
    remap_lat,
    remap_lon,
    pair_tile,
    pair_col,
    tile_owner,
    neighbours,
    land_mask,
    stem_w,
    dw_w,
    ln_gain,
    w_in,
    b_in,
    w_out,
    head_w,
):
    n = side
    group = n * CORES
    pairs = pair_col.shape[0]
    operands = (
        tile_owner[None],
        pair_tile.T,
        pair_col[None],
        neighbours.T,
        atmos,
        remap_lon.transpose(1, 2, 0),
        remap_lat.transpose(1, 2, 0),
        stem_w,
        dw_w,
        b_in,
        ln_gain[None],
        head_w[None],
        w_in,
        w_out,
        land_mask,
    )
    vmem = pltpu.VMEM
    dma = pltpu.SemaphoreType.DMA
    frows = 38 * 16
    return pl.pallas_call(
        functools.partial(kernel, n),
        out_shape=jax.ShapeDtypeStruct((2, 4096), F32),
        in_specs=[pl.BlockSpec(memory_space=pl.ANY)] * 15,
        out_specs=pl.BlockSpec(memory_space=vmem),
        scratch_shapes=[vmem(a.shape, a.dtype) for a in operands]
        + [
            dma((15,)),
            vmem((16, 1536), F32),
            vmem((512, 1536), BF16),
            vmem((16, 256), F32),
            vmem((16, 256), BF16),
            vmem((2, 32, 128), F32),
            vmem((2, 64, 128), F32),
            vmem((NX, 8, 256), F32),
            vmem((32, 16, pairs), F32),
            vmem((4, 256, pairs), BF16),
            vmem((2 * group, 4, 2 * n, 256), BF16),
            vmem((2, group, 4, 2 * n, 256), BF16),
            vmem((2, n, 96, 128), BF16),
            vmem((2, n, 96, 128), BF16),
            vmem((2, 64, 192), BF16),
            vmem((192, 64), BF16),
            vmem((2, 32, 128), BF16),
            vmem((2, group, 32, 128), BF16),
            vmem((2, 2, n * NX * 16, group * 32), BF16),
            vmem((2, n, NX, 16, 128), BF16),
            vmem((2, NX * n, 16, 128), BF16),
            vmem((frows, 64), BF16),
            vmem((NX, 48, 192), BF16),
            vmem((640, 128), BF16),
            vmem((frows, 640), BF16),
            vmem((2, frows, 128), BF16),
            vmem((frows, 128), BF16),
            vmem((37, 7, 16, 128), BF16),
            vmem((256, 896), BF16),
            vmem((NX, 192, 192), BF16),
            vmem((NX, 192, 192), BF16),
            vmem((48, 784), BF16),
            vmem((NX, 48, 784), BF16),
            vmem((48, 16), BF16),
            vmem((NX, 48, 16), BF16),
            vmem((NX, 16, 256), BF16),
            vmem((768, 192), BF16),
            vmem((768, 128), F32),
            vmem((768, 128), F32),
            vmem((192, 128), F32),
            vmem((8, 1, 256), F32),
            dma((2,)),
            dma((2,)),
            dma((2,)),
            dma((2,)),
            dma((2,)),
            dma((2,)),
            dma((1,)),
            dma((1,)),
            dma((2,)),
            dma((2,)),
            dma((5,)),
            dma((5,)),
            dma((1,)),
            dma((1,)),
        ],
        compiler_params=pltpu.CompilerParams(
            collective_id=0, has_side_effects=True, vmem_limit_bytes=56 * 1024 * 1024
        ),
        cost_estimate=pl.CostEstimate(flops=4000000000, bytes_accessed=4000000, transcendentals=2000000),
    )(*operands)


def solution(mesh):
    side = 1
    while side * side * CORES < mesh.shape["band"]:
        side *= 2
    return jax.shard_map(
        functools.partial(body, side),
        mesh=mesh,
        in_specs=(
            P("chan", "band", None),
            P("band", None, None),
            P("band", None, None),
            P("band", None),
            P("band"),
            P(),
            P(),
            P("band", None),
            P(None, "chan"),
            P("chan", None),
            P("chan"),
            P("chan", None),
            P("chan"),
            P("chan", None),
            P("chan"),
        ),
        out_specs=P("band", None),
        check_vma=False,
    )
```

```python
import functools

import jax
import jax.numpy as jnp
from jax import lax
from jax.experimental import pallas as pl
from jax.experimental.pallas import tpu as pltpu
from jax.sharding import PartitionSpec as P

MESH = pl.DeviceIdType.MESH
F32 = jnp.float32
BF16 = jnp.bfloat16
NX = 4
CORES = 2


def iota(shape, axis):
    return lax.broadcasted_iota(jnp.int32, shape, axis)


def onehot(mask):
    return jnp.where(mask, 1.0, 0.0).astype(BF16)


def mm(a, b):
    return lax.dot_general(a, b, (((1,), (0,)), ((), ())), preferred_element_type=F32)


def mm_nt(a, b):
    return lax.dot_general(a, b, (((1,), (1,)), ((), ())), preferred_element_type=F32)


def mm_tn(a, b):
    return lax.dot_general(a, b, (((0,), (0,)), ((), ())), preferred_element_type=F32)


def sdiv(a, b):
    return lax.div(a, jnp.int32(b))


def third(v):
    return jnp.where(v >= 6, 2, jnp.where(v >= 3, 1, 0))


def kernel(
    side,
    owner_hbm,
    tile_hbm,
    col_hbm,
    near_hbm,
    atm_hbm,
    lon_hbm,
    lat_hbm,
    stem_hbm,
    dw_hbm,
    b_in_hbm,
    gain_hbm,
    head_hbm,
    w_in_hbm,
    w_out_hbm,
    mask_hbm,
    out,
    owner_ref,
    tile_ref,
    col_ref,
    near_ref,
    atm,
    lon,
    lat,
    stem_w,
    dw_w,
    b_in,
    ln_gain,
    head_w,
    w_in,
    w_out,
    mask_ref,
    in_sems,
    arow,
    ashift,
    small_f,
    small,
    mrows_ref,
    mask,
    cells,
    xw,
    pls,
    send,
    recv,
    agg,
    part,
    flux,
    stacked,
    strips,
    gath,
    kmats,
    kwe,
    msgs,
    rb,
    edge_sel,
    fx,
    dmat,
    smat,
    rowsel,
    yx,
    zbuf,
    shift_all,
    w_all,
    o_all,
    c_loc,
    c_all,
    s_loc,
    s_all,
    sm_all,
    winp,
    bcol,
    vcol,
    hcol,
    res,
    p1_send,
    p1_recv,
    p2_send,
    p2_recv,
    a_send,
    a_recv,
    x_send,
    x_recv,
    b_send,
    b_recv,
    w_send,
    w_recv,
    f_send,
    f_recv,
):
    n = side
    group = n * CORES
    band = lax.axis_index("band")
    x = lax.axis_index("chan")
    y = sdiv(band, group)
    zc = lax.rem(band, group)
    z = sdiv(zc, CORES)
    c = lax.rem(zc, CORES)
    mine = (zc, y * CORES + c)
    ring = (y, z)

    def band_at(yy, zz, cc):
        return (yy * n + zz) * CORES + cc

    def group_band(k, idx):
        if k == 0:
            return y * group + idx
        return band_at(sdiv(idx, CORES), z, lax.rem(idx, CORES))

    def ring_band(k, t):
        return band_at(t, z, c) if k == 0 else band_at(y, t, c)

    def remote(src, dst, ssem, rsem, tb, tx):
        return pltpu.make_async_remote_copy(
            src_ref=src,
            dst_ref=dst,
            send_sem=ssem,
            recv_sem=rsem,
            device_id={"band": tb, "chan": tx},
            device_id_type=MESH,
        )

    def settle(ref, sem):
        pltpu.make_async_copy(ref, ref, sem).wait()

    loads = [
        pltpu.make_async_copy(src, dst, in_sems.at[i])
        for i, (src, dst) in enumerate(
            (
                (owner_hbm, owner_ref),
                (tile_hbm, tile_ref),
                (col_hbm, col_ref),
                (near_hbm, near_ref),
                (atm_hbm, atm),
                (lon_hbm, lon),
                (lat_hbm, lat),
                (stem_hbm, stem_w),
                (dw_hbm, dw_w),
                (b_in_hbm, b_in),
                (gain_hbm, ln_gain),
                (head_hbm, head_w),
                (w_in_hbm, w_in),
                (w_out_hbm, w_out),
                (mask_hbm, mask_ref),
            )
        )
    ]
    for load in loads:
        load.start()

    barrier = pltpu.get_barrier_semaphore()

    def greet(tb, tx):
        pl.semaphore_signal(
            barrier, inc=1, device_id={"band": tb, "chan": tx}, device_id_type=MESH
        )

    @pl.loop(1, group)
    def _(d):
        greet(y * group + lax.rem(zc + d, group), x)

    @pl.loop(1, n)
    def _(d):
        yy = lax.rem(y + d, n)
        greet(band_at(yy, z, 0), x)
        greet(band_at(yy, z, 1), x)

    @pl.loop(1, NX)
    def _(dx):
        xx = lax.rem(x + dx, NX)
        greet(band, xx)

        @pl.loop(1, n)
        def _(d):
            greet(band_at(lax.rem(y + d, n), z, c), xx)
            greet(band_at(y, lax.rem(z + d, n), c), xx)

    pairs = lon.shape[2]
    tiles = pairs
    lons = atm.shape[2]
    padded = arow.shape[1]
    arow[...] = jnp.zeros(arow.shape, F32)
    for i in range(5):
        loads[i].wait()
    for f in range(3):
        arow[4 * f : 4 * f + 4, 0:lons] = atm[f].astype(F32)
    row = arow[...]
    for i in range(32):
        moved = row if i == 0 else pltpu.roll(row, padded - i, 1)
        ashift[16 * i : 16 * i + 16, :] = moved.astype(BF16)
    owner = owner_ref[...]
    tile = tile_ref[...]
    col = col_ref[...]
    at_col = onehot(iota((padded, pairs), 0) == col)
    xw[...] = mm(ashift[...], at_col).reshape(32, 16, pairs)
    loads[5].wait()
    loads[6].wait()

    half = min(128, pairs)
    for ph in range(pairs // half):
        for jb in range(2):

            def step(ci, accs):
                block = lon[ci, jb * 32 : jb * 32 + 32, ph * half : (ph + 1) * half].astype(F32)
                return tuple(
                    accs[fr] + xw[ci, fr : fr + 1, ph * half : (ph + 1) * half] * block
                    for fr in range(12)
                )

            accs = lax.fori_loop(
                0, 32, step, tuple(jnp.zeros((32, half), F32) for _ in range(12)), unroll=4
            )
            for f in range(3):
                for r in range(4):
                    pls[r, f * 64 + jb * 32 : f * 64 + jb * 32 + 32, ph * half : (ph + 1) * half] = (
                        accs[f * 4 + r].astype(BF16)
                    )
    for r in range(4):
        pls[r, 192:256, :] = lat[:, r, :]

    ti = iota((tiles, pairs), 0)
    named = onehot(ti == tile)
    owner16 = jnp.broadcast_to(owner, (16, tiles)).astype(F32).astype(BF16)
    place = mm(owner16, named)[0:1, :].astype(jnp.int32)
    same = mm_tn(named, named)
    earlier = iota((pairs, pairs), 0) < iota((pairs, pairs), 1)
    rank = jnp.sum(jnp.where(earlier, same, 0.0), axis=0, keepdims=True).astype(jnp.int32)
    kk = lax.rem(place, 2)
    to_band = place // 2
    to_y = to_band // group
    to_zc = lax.rem(to_band, group)
    to_z = to_zc // CORES
    to_c = lax.rem(to_zc, CORES)
    slot = jnp.where(
        kk == 0,
        (to_zc * n + to_y) * 2 + rank,
        ((group + to_y * CORES + to_c) * n + to_z) * 2 + rank,
    )
    slots = 2 * group * n * 2
    perm = onehot(iota((slots, pairs), 0) == slot)
    for r in range(4):
        send[:, r] = mm_nt(perm, pls[r]).astype(BF16).reshape(2 * group, 2 * n, 256)

    greetings = (group - 1) + 2 * (n - 1) + 3 * (2 * n - 1)
    pl.semaphore_wait(barrier, greetings)

    def p1(k, d):
        idx = lax.rem(mine[k] + d, group)
        return remote(
            send.at[k * group + idx],
            recv.at[k, mine[k]],
            p1_send.at[k],
            p1_recv.at[k],
            group_band(k, idx),
            x,
        )

    @pl.loop(1, group)
    def _(d):
        p1(0, d).start()
        p1(1, d).start()

    for k in range(2):
        recv[k, mine[k]] = send[k * group + mine[k]]

    for i in range(7, 15):
        loads[i].wait()
    small_f[...] = jnp.zeros(small_f.shape, F32)
    small_f[0:1, 0:192] = b_in[...].astype(F32).reshape(1, 192)
    small_f[1:2, 0:48] = ln_gain[...].astype(F32)
    small_f[2:3, 0:48] = head_w[...].astype(F32)
    small[...] = small_f[...].astype(BF16)
    wide = 49 * 16
    lane = iota((49, wide), 1)
    spread = onehot(iota((49, wide), 0) == lane // 16)
    fields = onehot(iota((12, wide), 0) == lax.rem(iota((12, wide), 1), 16))
    combined = mm(dw_w[...], spread) * mm_tn(stem_w[...], fields)
    c_loc[...] = combined.astype(BF16)
    s_loc[...] = mm_tn(stem_w[...], onehot(iota((12, 16), 0) == iota((12, 16), 1))).astype(BF16)
    shares = ((w_in, w_all), (w_out, o_all), (c_loc, c_all), (s_loc, s_all), (small, sm_all))

    def share(i, dx):
        src, dst = shares[i]
        xx = lax.rem(x + dx, NX)
        return remote(src, dst.at[x], w_send.at[i], w_recv.at[i], band, xx)

    for dx in range(1, NX):
        for i in (4, 2, 3, 1, 0):
            share(i, dx).start()
    for src, dst in shares:
        dst[x] = src[...]

    ui = iota((tiles, tiles), 0)
    owner1 = jnp.broadcast_to(owner + 1, (16, tiles)).astype(F32).astype(BF16)
    near_rows = [mm(owner1, onehot(ui == near_ref[s : s + 1, :]))[0:1, :] for s in range(4)]
    near = jnp.concatenate(near_rows + [jnp.zeros((12, tiles), F32)], axis=0).astype(BF16)
    near_at = mm_nt(near, onehot(ui == owner)).astype(BF16)
    mrows = n * NX * 16
    mcols = group * 16
    mr = iota((mrows, tiles), 0)
    mt, mx = mr // 64, lax.rem(mr // 16, NX)
    ci = iota((mrows, mcols), 1)
    rho = lax.rem(iota((mrows, mcols), 0), 16)
    to_h = lax.rem(iota((mrows, mcols), 0) // 16, 2)
    src, src_rho = ci // 16, lax.rem(ci, 16)
    for k in range(2):
        to_place = 2 * (ring_band(k, mt)) + mx // 2
        cols = mm_nt(onehot(iota((mrows, tiles), 1) == to_place), near_at).astype(jnp.int32)
        if k == 0:
            src_place = 2 * (y * group + src)
        else:
            src_place = 2 * band_at(src // CORES, z, lax.rem(src, CORES)) + 1
        src_tag = jnp.where(src_rho == rho, src_place + 1, -1)
        col_ns = jnp.where(to_h == 0, cols[:, 0:1], cols[:, 1:2])
        col_we = jnp.where(rho < 9, cols[:, 2:3], cols[:, 3:4])
        ns = onehot(col_ns == src_tag).reshape(n, 2, 2, 16, mcols)
        for hh in range(2):
            kmats[k, hh] = ns[:, :, hh].reshape(mrows // 2, mcols)
        kwe[k] = onehot(col_we == src_tag)

    for k in range(2):
        for i in range(32):
            mrows_ref[k, i : i + 1, :] = mask_ref[k : k + 1, 128 * i : 128 * i + 128].astype(F32)
        for i in range(16):
            cells[2 * k + i // 8, i % 8 : i % 8 + 1, :] = mask_ref[
                k : k + 1, 256 * i : 256 * i + 256
            ].astype(F32)
        mpick = onehot(iota((64, 32), 1) == iota((64, 32), 0) // 2)
        mfull = mm(mpick, mrows_ref[k].astype(BF16))
        mswap = pltpu.roll(mfull, 64, 1)
        meven = lax.rem(iota((64, 128), 0), 2) * 64 + iota((64, 128), 1)
        keep = (meven < 64) | (meven >= 128)
        mask[k] = jnp.where(keep, mfull, mswap)

    h = lax.rem(x, 2)
    frows = 38 * 16
    fr_row = iota((frows, 640), 0)
    r_row, f_row = fr_row // 16, lax.rem(fr_row, 16)
    fx_row = f_row // 3
    fl_row = f_row - 3 * fx_row
    strip_a = jnp.where(h == 0, r_row, r_row - 35)
    in_strip = (strip_a >= 0) & (strip_a <= 2)
    want = jnp.where(
        in_strip,
        576 + fx_row * 16 + fl_row * 3 + strip_a,
        f_row * 48 + jnp.where(h == 0, r_row - 3, r_row + 13),
    )
    smat[...] = onehot((want == iota((frows, 640), 1)) & (f_row < 12) & (want < 576))
    er_row, er_f = iota((frows, 64), 0) // 16, lax.rem(iota((frows, 64), 0), 16)
    er_a = jnp.where(h == 0, er_row, er_row - 35)
    er_to = er_f // 3 * 16 + lax.rem(er_f, 3) * 3 + er_a
    edge_sel[...] = onehot(
        (er_to == iota((frows, 64), 1)) & (er_f < 12) & (er_a >= 0) & (er_a <= 2)
    )
    rr = iota((frows, 128), 0) // 16
    ff = lax.rem(iota((frows, 128), 0), 16)
    ll = iota((frows, 128), 1)
    cell = rr - 3 + 32 * h
    rowsel[0] = onehot((cell == lax.rem(ll, 64)) & (cell >= 0) & (cell < 64))
    lo = ll < 64
    lx, lrho = lax.rem(ll, 64) // 16, lax.rem(ll, 16)
    fa = jnp.where(lo, lrho - 9, jnp.where(lrho < 9, lrho, lrho - 2))
    ok = (lo & (lrho >= 9)) | (jnp.logical_not(lo) & (lrho < 11))
    rowsel[1] = onehot(ok & (3 * lx + third(fa) == ff))
    kr = iota((128, 128), 0)
    klo = kr < 64
    krho = lax.rem(kr, 16)
    kfa = jnp.where(klo, krho - 9, jnp.where(krho < 9, krho, krho - 2))
    kwest = jnp.logical_not(klo) & (krho < 9)
    lane_to = jnp.where(kwest, 64, 67) + kfa - 3 * third(kfa)
    collapse = onehot(lane_to == iota((128, 128), 1))
    ar = iota((256, 896), 0)
    al = lax.rem(ar, 128)
    ncol = jnp.where(al < 64, al + 3, jnp.where(al < 67, al - 64, jnp.where(al < 70, al, -999)))
    bc = iota((256, 896), 1)
    shift_all[...] = onehot(
        (ar // 128 == lax.rem(bc, 128) // 64) & (ncol == lax.rem(bc, 64) + bc // 128)
    )
    dmat[...] = jnp.zeros(dmat.shape, BF16)
    sr = iota((32, 192), 0)
    sl = iota((32, 192), 1)
    srho = lax.rem(sr, 16)
    sfl = third(srho)
    sa = srho - 3 * sfl
    pick_rows = onehot(
        (srho < 9) & (sl // 64 == sfl) & (lax.rem(sl, 64) == sa + jnp.where(sr < 16, 61, 0))
    )
    er = iota((48, 192), 0)
    el = iota((48, 192), 1)
    erho = lax.rem(er, 16)
    efa = jnp.where(er < 16, erho, jnp.where(er < 32, erho - 9, erho - 2))
    eok = (
        ((er < 16) & (erho < 9))
        | ((er >= 16) & (er < 32) & (erho >= 9))
        | ((er >= 32) & (erho >= 9) & (erho < 11))
    )
    efl = third(efa)
    ea = efa - 3 * efl + jnp.where(er < 16, 61, 0)
    pick_cols = onehot(eok & (el // 64 == efl) & (lax.rem(el, 64) == ea))

    def p2(k, d):
        t = lax.rem(ring[k] + d, n)
        return remote(
            agg.at[k, t],
            part.at[k, ring[k]],
            p2_send.at[k],
            p2_recv.at[k],
            ring_band(k, t),
            x,
        )

    krows = group * 8 * n
    k_tile = lax.rem(iota((64, krows), 1) // 2, n)
    for k in range(2):

        settle(recv.at[k, pl.ds(0, group - 1)], p1_recv.at[k])

        got = recv[k].reshape(krows, 256)
        lat_t = got[:, 128:256].astype(F32).T[64:128, :]
        lhs = jnp.concatenate(
            [jnp.where(k_tile == t, lat_t, 0.0).astype(BF16) for t in range(n)], axis=0
        )
        sums = mm(lhs, got[:, 0:192])
        agg[k, :, 0:64, :] = sums[:, 0:128].astype(BF16).reshape(n, 64, 128)
        last = sums[:, 128:192].reshape(n, 2, 32, 64)
        agg[k, :, 64:96, :] = jnp.concatenate([last[:, 0], last[:, 1]], axis=2).astype(BF16)

        @pl.loop(1, n)
        def _(d):
            p2(k, d).start()

        part[k, ring[k]] = agg[k, ring[k]]

    def xcopy(dx):
        xx = lax.rem(x + dx, NX)
        at = pl.multiple_of(16 * lax.rem(xx, 2), 16)
        return remote(
            flux.at[sdiv(xx, 2), pl.ds(at, 48)], fx.at[x], x_send.at[0], x_recv.at[0], band, xx
        )

    def acopy(k, d):
        idx = lax.rem(mine[k] + d, group)
        return remote(
            strips.at[k],
            gath.at[k, mine[k]],
            a_send.at[k],
            a_recv.at[k],
            group_band(k, idx),
            x,
        )

    for k in range(2):

        settle(part.at[k, pl.ds(0, n - 1)], p2_recv.at[k])

        total = part[k, 0].astype(F32)
        for t in range(1, n):
            total = total + part[k, t].astype(F32)
        last = jnp.concatenate([total[64:96, 0:64], total[64:96, 64:128]], axis=0)
        masked = [total[0:64, :] * mask[k], last * mask[k, :, 0:64]]
        tile_flux = jnp.concatenate(masked, axis=1).astype(BF16)
        flux[k] = tile_flux
        for f in range(3):
            stacked[f * 64 : f * 64 + 64, :] = tile_flux[:, f * 64 : f * 64 + 64]
        ns = mm(pick_rows, stacked[...])
        we = mm_nt(pick_cols, tile_flux)
        strips[k, 0:16, :] = jnp.concatenate([ns[0:16], we[0:16]], axis=1).astype(BF16)
        strips[k, 16:32, :] = jnp.concatenate([ns[16:32] + we[16:32], we[32:48]], axis=1).astype(
            BF16
        )

        @pl.loop(1, group)
        def _(d):
            acopy(k, d).start()

        gath[k, mine[k]] = strips[k]

    for dx in range(1, NX):
        xcopy(dx).start()
    fx[x] = flux[sdiv(x, 2), pl.ds(pl.multiple_of(16 * h, 16), 48), :]

    def bcopy(k, t, xx):
        return remote(
            msgs.at[k, t, xx],
            rb.at[k, x * n + ring[k]],
            b_send.at[k],
            b_recv.at[k],
            ring_band(k, t),
            xx,
        )

    def each_b(k, fn):
        @pl.loop(1, NX)
        def _(dx):
            fn(k, ring[k], lax.rem(x + dx, NX))

        @pl.loop(1, n)
        def _(d):
            for dx in range(NX):
                fn(k, lax.rem(ring[k] + d, n), lax.rem(x + dx, NX))

    low = iota((mrows, 128), 1) < 64
    body_rows = lax.rem(iota((mrows, 128), 0), 16) < 9
    for k in range(2):

        settle(gath.at[k, pl.ds(0, group - 1)], a_recv.at[k])

        near_s = gath[k, :, 0:16, :]
        near_n = gath[k, :, 16:32, :]
        top = iota((group, 16, 128), 1) < 9
        mixed_we = jnp.where(top, near_s.astype(F32), near_n.astype(F32)).astype(BF16)
        from_we = mm(kwe[k], mixed_we.reshape(mcols, 128))
        from_ns = [
            mm(kmats[k, hh], part_ns.reshape(mcols, 128)).reshape(n, 2, 16, 128)
            for hh, part_ns in enumerate((near_s, near_n))
        ]
        from_ns = jnp.stack(from_ns, axis=2).reshape(mrows, 128)
        msg = jnp.where(low & body_rows, from_ns, from_we)
        msgs[k] = msg.astype(BF16).reshape(n, NX, 16, 128)
        each_b(k, lambda k, t, xx: bcopy(k, t, xx).start())
        rb[k, x * n + ring[k]] = msgs[k, ring[k], x]

    for i, (_, dst) in enumerate(shares):
        settle(dst.at[pl.ds(0, NX - 1)], w_recv.at[i])
    gains = jnp.zeros((16, 192), F32)
    for i in range(NX):
        put = onehot(iota((256, 192), 1) == jnp.where(iota((256, 192), 0) < 48, iota((256, 192), 0) + 48 * i, -1))
        gains = gains + mm(sm_all[i], put)
    row2 = onehot(iota((16, 128), 0) == 2)
    row0 = onehot(iota((16, 128), 0) == 0)
    head = mm_tn(gains.astype(BF16), row2)
    hcol[...] = head
    for i in range(NX):
        blk = pl.ds(i * 192, 192)
        winp[blk, :] = (w_all[i].astype(F32) * gains[1:2, :]).astype(BF16)
        bcol[blk, :] = mm_tn(sm_all[i, :, 0:192], row0)
        vcol[blk, :] = 0.5 * mm(o_all[i], head.astype(BF16))

    settle(fx.at[pl.ds(0, NX - 1)], x_recv.at[0])
    for f in range(12):
        dmat[f * 48 : f * 48 + 48, 0:64] = fx[f // 3, :, (f % 3) * 64 : (f % 3) * 64 + 64]
    yx[...] = mm(smat[...], dmat[...]).astype(BF16)
    for k in range(2):
        settle(rb.at[k, pl.ds(0, NX * n - 1)], b_recv.at[k])
    total = jnp.zeros((NX, 16, 128), F32)
    for k in range(2):
        arrived = rb[k].reshape(NX, n, 16, 128)
        for t in range(n):
            total = total + arrived[:, t].astype(F32)
    edge = total.reshape(64, 128)
    elow = iota((64, 128), 1) < 64
    edge_low = jnp.where(elow, edge, 0.0)
    both = jnp.concatenate([edge_low, jnp.where(elow, 0.0, edge)], axis=0)
    picked = mm_nt(rowsel[0], both.astype(BF16)) * rowsel[1].astype(F32)
    outer_rows = mm(edge_sel[...], edge_low.astype(BF16)) + mm(picked.astype(BF16), collapse)
    yx[...] = (yx[...].astype(F32) + outer_rows).astype(BF16)
    pair_rows = jnp.concatenate([yx[0:592, :], yx[16:608, :]], axis=1)
    for b in range(7):
        zbuf[:, b] = (
            mm(pair_rows, shift_all[:, b * 128 : b * 128 + 128]).astype(BF16).reshape(37, 16, 128)
        )

    @pl.loop(0, 8, unroll=2)
    def _(i):
        left = zbuf[pl.ds(4 * i, 7)].reshape(wide, 128)
        right = zbuf[pl.ds(4 * i + 2, 7)].reshape(wide, 128)
        mixed = mm(c_all[...].reshape(192, wide), jnp.concatenate([left, right], axis=1))
        mean = jnp.sum(mixed, axis=0, keepdims=True) * (1.0 / 192.0)
        sq = jnp.sum(mixed * mixed, axis=0, keepdims=True) * (1.0 / 192.0)
        scale = lax.rsqrt(sq - mean * mean + 1e-06)
        normed = ((mixed - mean) * scale).astype(BF16)
        centre = jnp.concatenate([zbuf[4 * i + 3, 3], zbuf[4 * i + 5, 3]], axis=1)
        inner = mm(s_all[...].reshape(192, 16), centre).astype(BF16).astype(F32)
        hc = jnp.concatenate([hcol[...], hcol[...]], axis=1)
        acc = jnp.sum(inner * hc, axis=0, keepdims=True)
        for q in range(6):
            blk = slice(q * 128, q * 128 + 128)
            bias = jnp.concatenate([bcol[blk, :], bcol[blk, :]], axis=1)
            vals = jnp.concatenate([vcol[blk, :], vcol[blk, :]], axis=1)
            pre = mm(winp[blk, :], normed) + bias
            inside = pre * (0.7978845608 + (0.7978845608 * 0.044715) * (pre * pre))
            acc = acc + jnp.sum(vals * (pre * (1.0 + jnp.tanh(inside))), axis=0, keepdims=True)
        res[i] = acc

    out[x] = jnp.concatenate([res[i] for i in range(8)], axis=0) * cells[x]

    def fcopy(dx):
        xx = lax.rem(x + dx, NX)
        return remote(out.at[x], out.at[x], f_send.at[0], f_recv.at[0], band, xx)

    for dx in range(1, NX):
        fcopy(dx).start()

    for k in range(2):
        settle(send.at[pl.ds(0, group - 1)], p1_send.at[k])
        settle(part.at[k, pl.ds(0, n - 1)], p2_send.at[k])
        settle(gath.at[k, pl.ds(0, group - 1)], a_send.at[k])
        settle(rb.at[k, pl.ds(0, NX * n - 1)], b_send.at[k])
    settle(fx.at[pl.ds(0, NX - 1)], x_send.at[0])
    for i, (_, dst) in enumerate(shares):
        settle(dst.at[pl.ds(0, NX - 1)], w_send.at[i])
    settle(out.at[pl.ds(0, NX - 1)], f_send.at[0])
    settle(out.at[pl.ds(0, NX - 1)], f_recv.at[0])


def body(
    side,
    atmos,
    remap_lat,
    remap_lon,
    pair_tile,
    pair_col,
    tile_owner,
    neighbours,
    land_mask,
    stem_w,
    dw_w,
    ln_gain,
    w_in,
    b_in,
    w_out,
    head_w,
):
    n = side
    group = n * CORES
    pairs = pair_col.shape[0]
    operands = (
        tile_owner[None],
        pair_tile.T,
        pair_col[None],
        neighbours.T,
        atmos,
        remap_lon.transpose(1, 2, 0),
        remap_lat.transpose(1, 2, 0),
        stem_w,
        dw_w,
        b_in,
        ln_gain[None],
        head_w[None],
        w_in,
        w_out,
        land_mask,
    )
    vmem = pltpu.VMEM
    dma = pltpu.SemaphoreType.DMA
    frows = 38 * 16
    result = pl.pallas_call(
        functools.partial(kernel, n),
        out_shape=jax.ShapeDtypeStruct((NX, 8, 256), F32),
        in_specs=[pl.BlockSpec(memory_space=pl.ANY)] * 15,
        out_specs=pl.BlockSpec(memory_space=vmem),
        scratch_shapes=[vmem(a.shape, a.dtype) for a in operands]
        + [
            dma((15,)),
            vmem((16, 1536), F32),
            vmem((512, 1536), BF16),
            vmem((16, 256), F32),
            vmem((16, 256), BF16),
            vmem((2, 32, 128), F32),
            vmem((2, 64, 128), F32),
            vmem((NX, 8, 256), F32),
            vmem((32, 16, pairs), F32),
            vmem((4, 256, pairs), BF16),
            vmem((2 * group, 4, 2 * n, 256), BF16),
            vmem((2, group, 4, 2 * n, 256), BF16),
            vmem((2, n, 96, 128), BF16),
            vmem((2, n, 96, 128), BF16),
            vmem((2, 64, 192), BF16),
            vmem((192, 64), BF16),
            vmem((2, 32, 128), BF16),
            vmem((2, group, 32, 128), BF16),
            vmem((2, 2, n * NX * 8, group * 16), BF16),
            vmem((2, n * NX * 16, group * 16), BF16),
            vmem((2, n, NX, 16, 128), BF16),
            vmem((2, NX * n, 16, 128), BF16),
            vmem((frows, 64), BF16),
            vmem((NX, 48, 192), BF16),
            vmem((640, 128), BF16),
            vmem((frows, 640), BF16),
            vmem((2, frows, 128), BF16),
            vmem((frows, 128), BF16),
            vmem((37, 7, 16, 128), BF16),
            vmem((256, 896), BF16),
            vmem((NX, 192, 192), BF16),
            vmem((NX, 192, 192), BF16),
            vmem((48, 784), BF16),
            vmem((NX, 48, 784), BF16),
            vmem((48, 16), BF16),
            vmem((NX, 48, 16), BF16),
            vmem((NX, 16, 256), BF16),
            vmem((768, 192), BF16),
            vmem((768, 128), F32),
            vmem((768, 128), F32),
            vmem((192, 128), F32),
            vmem((8, 1, 256), F32),
            dma((2,)),
            dma((2,)),
            dma((2,)),
            dma((2,)),
            dma((2,)),
            dma((2,)),
            dma((1,)),
            dma((1,)),
            dma((2,)),
            dma((2,)),
            dma((5,)),
            dma((5,)),
            dma((1,)),
            dma((1,)),
        ],
        compiler_params=pltpu.CompilerParams(
            collective_id=0, has_side_effects=True, vmem_limit_bytes=56 * 1024 * 1024
        ),
        cost_estimate=pl.CostEstimate(flops=4000000000, bytes_accessed=4000000, transcendentals=2000000),
    )(*operands)
    return result.reshape(2, 4096)


def solution(mesh):
    side = 1
    while side * side * CORES < mesh.shape["band"]:
        side *= 2
    return jax.shard_map(
        functools.partial(body, side),
        mesh=mesh,
        in_specs=(
            P("chan", "band", None),
            P("band", None, None),
            P("band", None, None),
            P("band", None),
            P("band"),
            P(),
            P(),
            P("band", None),
            P(None, "chan"),
            P("chan", None),
            P("chan"),
            P("chan", None),
            P("chan"),
            P("chan", None),
            P("chan"),
        ),
        out_specs=P("band", None),
        check_vma=False,
    )
```
